512 devices in a mesh: row: 16 (over z, core), col: 32 (over y, x).
Axes of the slice: x: 4, y: 8, z: 8, core: 2. Of those that a mesh axis runs over, the one named last changes fastest.
Arguments:
- velocity: bfloat16 [3, 4, 4224, 4096], P(None, None, 'row', 'col'), may hold values from -6 to 6
- rhs_prev: bfloat16 [3, 4, 4224, 4096], P(None, None, 'row', 'col'), may hold values from -12 to 12
- row_counts: int32 [16], replicated, may hold values from 248 to 264, as said below
- x_scale: float32 [4096], P('col'), may hold values from 0.5 to 2
- x_curv: float32 [4096], P('col'), may hold values from -3 to 3
- y_scale: float32 [4224], P('row'), may hold values from 0.5 to 12
- y_curv: float32 [4224], P('row'), may hold values from -3 to 3
- x_local: bfloat16 [132, 2, 128], replicated, may hold values from -0.5 to 0.5
- x_coupling: float32 [2, 64, 64], replicated, may hold values from -0.75 to 0.75
- x_basis: float32 [2, 2, 128], replicated, may hold values from -3 to 3
- y_local: bfloat16 [4288, 2, 264], P('row'), may hold values from -0.375 to 0.375
- y_coupling: float32 [2, 32, 32], replicated, may hold values from -1 to 1
- y_basis: float32 [16, 2, 2, 264], P('row'), may hold values from -3 to 3
Outputs:
- rhs: bfloat16 [3, 4, 4224, 4096], P(None, None, 'row', 'col')
- increment: bfloat16 [3, 4, 4224, 4096], P(None, None, 'row', 'col')
The draws below stay inside these ranges and needn't reach their ends.
Inputs may be any that keep to these rules, and one draw needn't show every extreme that they name: `row_counts`: the counts sum to 4097; each is at least 2, and the largest is exactly 264.
All inputs are finite; a program needn't handle non-finite values.
Results may differ from the reference program's by a relative error of at most 0.0055.
Values may be sent and summed in bfloat16 or wider, within the bound.
No kernel may reach another device: no remote copies, remote signals or barrier semaphores. Data moves between devices by JAX's collectives and lax.ppermute only.
A program may use at most 64 MiB of HBM per device.

```python
import math
import jax
import jax.numpy as jnp
from jax import lax

NX = 4096
NY = 4097
ZW = 4
XB = 128
SKEW = 8
YB = 264
YP = 4224
N_ROW = 16
N_COL = 32


def draw_row_counts(key, part):
    base_rows = NY // N_ROW
    extra_rows = NY % N_ROW
    pick_key, roll_key = jax.random.split(jax.random.fold_in(key, 11))
    lift_ids = jax.random.randint(pick_key, (N_ROW,), 0, SKEW + 1)
    position = jnp.arange(N_ROW, dtype=jnp.int32)
    lift_ids = jnp.where(position == 0, SKEW, jnp.where(position == N_ROW - 1, 0, lift_ids))
    counts = base_rows + lift_ids - jnp.roll(lift_ids, 1) + jnp.where(position == 1, extra_rows, 0)
    roll_by = jax.random.randint(roll_key, (), 0, N_ROW)
    return jnp.roll(counts, roll_by).astype(jnp.int32)


def draw_y_scale(key, part):
    position = jnp.arange(YP, dtype=jnp.float32) / (YP - 1)
    jitter = jax.random.uniform(jax.random.fold_in(key, 5), (YP,), jnp.float32, 0.7, 1.3)
    return jnp.exp(jnp.log(4.0) * position) * jitter


def block_scale(rng, extent, pieces, smallest, high):
    loudness, own = 1.0, jax.random.fold_in(rng, 6)
    for dim, parts in pieces:
        heights = jnp.exp(jax.random.uniform(jax.random.fold_in(own, dim), (parts,), jnp.float32, smallest / len(pieces), high / len(pieces)))
        loudness = loudness * jnp.repeat(heights, extent[dim] // parts).reshape([-1 if axis == dim else 1 for axis in range(len(extent))])
    return loudness


def normal_values(rng, extent, width, limit, pieces=(), kind=jnp.bfloat16):
    factor_of = block_scale(rng, extent, pieces, -0.22, 0.18) if pieces else 1.0
    drawn = jax.random.normal(rng, extent, jnp.float32) * width * factor_of
    return jnp.minimum(jnp.maximum(drawn, -limit), limit).astype(kind)


def setup_inputs(seed: int = 0) -> dict:
    key_of = jax.random.split(jax.random.key(seed), 14)
    return {
        "velocity": normal_values(key_of[0], (3, ZW, YP, NX), 1.0, 6.0, ((2, 16), (3, 32))),
        "rhs_prev": normal_values(key_of[1], (3, ZW, YP, NX), 2.0, 12.0, ((2, 16), (3, 32))),
        "row_counts": draw_row_counts(jax.random.fold_in(key_of[13], 71), 0),
        "x_scale": jnp.clip(jnp.exp(math.log(2.0) - 1.3862944 * jax.random.uniform(key_of[3], (NX,), jnp.float32) ** block_scale(key_of[3], (NX,), ((0, 32),), -0.2, 0.2)), 0.5, 2.0),
        "x_curv": normal_values(key_of[4], (NX,), 0.5, 3.0, ((0, 32),), jnp.float32),
        "y_scale": draw_y_scale(jax.random.fold_in(key_of[13], 71), 0),
        "y_curv": normal_values(key_of[6], (YP,), 0.5, 3.0, ((0, 16),), jnp.float32),
        "x_local": normal_values(key_of[7], (XB + 4, 2, XB), (XB + 4) ** -0.5, 0.5),
        "x_coupling": normal_values(key_of[8], (2, 2 * N_COL, 2 * N_COL), (2 * N_COL) ** -0.5, 0.75, (), jnp.float32),
        "x_basis": normal_values(key_of[9], (2, 2, XB), 0.5, 3.0, (), jnp.float32),
        "y_local": normal_values(key_of[10], (N_ROW * (YB + 4), 2, YB), (YB + 4) ** -0.5, 0.375, ((0, 16),)),
        "y_coupling": normal_values(key_of[11], (2, 2 * N_ROW, 2 * N_ROW), (2 * N_ROW) ** -0.5, 1.0, (), jnp.float32),
        "y_basis": normal_values(key_of[12], (N_ROW, 2, 2, YB), 0.5, 3.0, ((0, 16),), jnp.float32),
    }


viscosity = 0.1
cfl_target = 1.5
gamma_coef = 5.0 / 12.0
zeta_coef = -17.0 / 60.0


def x_derivs(fields_in, x_local, x_coupling, x_basis):
    x_width = NX // N_COL
    starts = jnp.arange(N_COL, dtype=jnp.int32) * x_width - 2
    gather_ids = (starts[:, None] + jnp.arange(x_width + 4, dtype=jnp.int32)[None, :]) % NX
    extended = fields_in[:, :, gather_ids]
    local_terms = jnp.dot(extended.reshape(-1, x_width + 4), x_local.reshape(x_width + 4, 2 * x_width), preferred_element_type=jnp.float32)
    local_terms = local_terms.reshape(3, YP, N_COL, 2, x_width)
    ends_x = jnp.stack([local_terms[..., 0], local_terms[..., x_width - 1]], axis=-1)
    ends_x = jnp.transpose(ends_x, (0, 1, 3, 2, 4)).reshape(3, YP, 2, 2 * N_COL)
    solved = jnp.einsum('kim,cykm->cyki', x_coupling, ends_x, precision=lax.Precision.HIGHEST)
    solved = jnp.transpose(solved.reshape(3, YP, 2, N_COL, 2), (0, 1, 3, 2, 4))
    result = local_terms + solved[..., 0:1] * x_basis[:, 0, :] + solved[..., 1:2] * x_basis[:, 1, :]
    first_x = result[:, :, :, 0, :].reshape(3, YP, NX)
    second_x = result[:, :, :, 1, :].reshape(3, YP, NX)
    return first_x, second_x


def y_derivs(masked, row_counts, y_local, y_coupling, y_basis):
    y_rows = YB
    blocks = jnp.arange(N_ROW, dtype=jnp.int32)
    below_counts = jnp.roll(row_counts, 1)
    offsets = jnp.arange(y_rows + 4, dtype=jnp.int32)
    low_ids = (blocks[:, None] - 1) * y_rows + below_counts[:, None] - 2 + offsets[None, :]
    mid_ids = blocks[:, None] * y_rows + offsets[None, :] - 2
    high_ids = (blocks[:, None] + 1) * y_rows + offsets[None, :] - y_rows - 2
    gather_ids = jnp.where(offsets[None, :] < 2, low_ids, jnp.where(offsets[None, :] < y_rows + 2, mid_ids, high_ids))
    keep_low = jnp.logical_or(offsets[None, :] >= 2, blocks[:, None] > 0)
    keep_high = jnp.logical_or(offsets[None, :] < y_rows + 2, blocks[:, None] < N_ROW - 1)
    keep_ids = jnp.logical_and(keep_low, keep_high)
    gather_ids = jnp.clip(gather_ids, 0, YP - 1).astype(jnp.int32)
    extended = jnp.where(keep_ids[None, :, :, None], masked[:, gather_ids, :], jnp.zeros((), masked.dtype))
    weights = y_local.reshape(N_ROW, y_rows + 4, 2 * y_rows).astype(jnp.float32)
    local_terms = jnp.einsum('qem,cqex->cqmx', weights, extended.astype(jnp.float32))
    local_terms = local_terms.reshape(3, N_ROW, 2, y_rows, NX)
    first_rows = local_terms[:, :, :, 0, :]
    last_rows = jnp.moveaxis(local_terms[:, blocks, :, row_counts - 1, :], 0, 1)
    ends_y = jnp.stack([first_rows, last_rows], axis=3)
    ends_y = jnp.transpose(ends_y, (0, 2, 1, 3, 4)).reshape(3, 2, 2 * N_ROW, NX)
    solved = jnp.einsum('kim,ckmx->ckix', y_coupling, ends_y, precision=lax.Precision.HIGHEST)
    solved = jnp.transpose(solved.reshape(3, 2, N_ROW, 2, NX), (0, 2, 1, 3, 4))
    result = local_terms + solved[:, :, :, 0, :][:, :, :, None, :] * y_basis[None, :, :, 0, :, None] + solved[:, :, :, 1, :][:, :, :, None, :] * y_basis[None, :, :, 1, :, None]
    first_y = result[:, :, 0].reshape(3, YP, NX)
    second_y = result[:, :, 1].reshape(3, YP, NX)
    return first_y, second_y


def reference(velocity, rhs_prev, row_counts, x_scale, x_curv, y_scale, y_curv, x_local, x_coupling, x_basis, y_local, y_coupling, y_basis):
    slot_ids = jnp.arange(YP, dtype=jnp.int32)
    valid_rows = (slot_ids % YB) < row_counts[slot_ids // YB]
    speeds = jnp.abs(velocity[0].astype(jnp.float32)) * x_scale + jnp.abs(velocity[1].astype(jnp.float32)) * y_scale[:, None]
    speed_top = jnp.max(jnp.where(valid_rows[:, None], speeds, jnp.float32(0.0)))
    time_step = cfl_target / (speed_top + 1e-6)
    scale_x = x_scale
    curve_x = x_curv
    scale_y = y_scale[:, None]
    curve_y = y_curv[:, None]

    def one_plane(plane_args):
        fields_in, previous = plane_args
        masked = jnp.where(valid_rows[None, :, None], fields_in, jnp.zeros((), fields_in.dtype))
        first_x, second_x = x_derivs(fields_in, x_local, x_coupling, x_basis)
        first_y, second_y = y_derivs(masked, row_counts, y_local, y_coupling, y_basis)
        velocity_f = fields_in.astype(jnp.float32)
        grad_x = scale_x * first_x
        grad_y = scale_y * first_y
        laplacian = scale_x * scale_x * second_x + curve_x * first_x + scale_y * scale_y * second_y + curve_y * first_y
        rhs_full = -(velocity_f[0:1] * grad_x + velocity_f[1:2] * grad_y) + viscosity * laplacian
        rhs_full = jnp.where(valid_rows[None, :, None], rhs_full, jnp.float32(0.0))
        change = time_step * (gamma_coef * rhs_full + zeta_coef * previous.astype(jnp.float32))
        change = jnp.where(valid_rows[None, :, None], change, jnp.float32(0.0))
        return rhs_full.astype(jnp.bfloat16), change.astype(jnp.bfloat16)

    fields = jnp.moveaxis(velocity, 1, 0)
    previous_rhs = jnp.moveaxis(rhs_prev, 1, 0)
    totals, changes = lax.map(one_plane, (fields, previous_rhs))
    return jnp.moveaxis(totals, 0, 1), jnp.moveaxis(changes, 0, 1)
```

```python
import jax
import jax.numpy as jnp
from jax import lax
from jax.experimental import pallas as pl
from jax.experimental.pallas import tpu as pltpu
from jax.sharding import Mesh
from jax.sharding import PartitionSpec as P

COL = ("col_0", "col_1")
ROW = ("row_0", "row_1")

viscosity = 0.1
cfl_target = 1.5
gamma_coef = 5.0 / 12.0
zeta_coef = -17.0 / 60.0

F32 = jnp.float32
BF16 = jnp.bfloat16
NCOL = 32
NROW = 16
XW = 128
YR = 264
NP = 12
LINES = NP * YR
CHUNK = 112
CHUNKS = -(-LINES // CHUNK)
HALF = NP // 2
TILES = HALF + 1
EDGE_X = (0, 1, XW - 2, XW - 1)
HALO_X = (0, 1, XW + 2, XW + 3)


def nn(a, b, precision=None):
    return lax.dot_general(
        a, b, (((1,), (0,)), ((), ())), precision=precision, preferred_element_type=F32
    )


def nt(a, b):
    return lax.dot_general(a, b, (((1,), (1,)), ((), ())), preferred_element_type=F32)


def tn(a, b):
    return lax.dot_general(a, b, (((0,), (0,)), ((), ())), preferred_element_type=F32)


def iota(shape, dim):
    return lax.broadcasted_iota(jnp.int32, shape, dim)


def ones_where(cond):
    return jnp.where(cond, F32(1.0), F32(0.0))


def row_pos():
    return lax.axis_index("row_0") * 2 + lax.axis_index("row_1")


def three_parts(value):
    high = value.astype(BF16).astype(F32)
    rest = value - high
    mid = rest.astype(BF16).astype(F32)
    return high, mid, rest - mid


def max_tile(value):
    high, mid, low = three_parts(jnp.broadcast_to(value, (8, 128)))
    row = iota((8, 128), 0)
    return jnp.where(
        row == 0, high, jnp.where(row == 1, mid, jnp.where(row == 2, low, F32(0.0)))
    )


def column_tiles(row_ref, row):
    pieces = []
    for j in range(3):
        seg = row_ref[row : row + 1, 128 * j : 128 * j + 128]
        pieces.append(jnp.transpose(jnp.broadcast_to(seg, (128, 128))))
    return jnp.concatenate([pieces[0], pieces[1], pieces[2][0 : YR - 256]], axis=0)


def x_partial_kernel(v_ref, x_ref, o_ref):
    row, lane = iota((8, XW), 0), iota((8, XW), 1)
    pick = ones_where((row < 4) & (lane == (XW - 1) * (row % 2))).astype(BF16)
    ends = nt(pick, x_ref[...])
    row_e = iota((8, 2 * (XW + 4)), 0)
    weights = jnp.where(row == 4, ones_where(lane == EDGE_X[0]), F32(0.0))
    for j in range(1, 4):
        weights = jnp.where(row == 4 + j, ones_where(lane == EDGE_X[j]), weights)
    src, dst = iota((2 * (XW + 4), XW), 0), iota((2 * (XW + 4), XW), 1)
    for k in range(2):
        spread = ones_where(src == 2 * (dst + 2) + k).astype(BF16)
        mine = jnp.where((row_e // 2) == k, ends, F32(0.0)).astype(BF16)
        weights = weights + nn(mine, spread)
    weights = weights.astype(BF16)
    for d in range(NCOL):
        first = CHUNK * d
        if first + 128 <= LINES:
            o_ref[d] = nt(weights, v_ref[first : first + 128, :]).astype(BF16)
        elif first < LINES:
            part = nt(weights, v_ref[first:LINES, :])
            rest = jnp.zeros((8, 128 - (LINES - first)), F32)
            o_ref[d] = jnp.concatenate([part, rest], axis=1).astype(BF16)
        else:
            o_ref[d] = jnp.zeros((8, 128), BF16)


def y_partial_kernel(count_ref, v_ref, w_ref, xs_ref, ys_ref, o_ref, pad_ref):
    count = count_ref[row_pos()]
    row, slot = iota((8, YR), 0), iota((8, YR), 1)
    place = jnp.where(row % 2 == 0, 0, count - 1)
    ends = nn(ones_where((row < 2) & (slot == place)).astype(BF16), w_ref[0])
    ends = ends + nn(
        ones_where((row >= 2) & (row < 4) & (slot == place)).astype(BF16), w_ref[1]
    )
    pad_ref[...] = jnp.zeros_like(pad_ref)
    pad_ref[0:8, 0 : YR + 4] = ends
    pad_ref[8:9, 0:YR] = ys_ref[...]
    wide = pad_ref[0:8, :]
    own = pltpu.roll(wide, 384 - 2, 1)[:, 0:YR]
    edge = jnp.where(
        row == 4, 0, jnp.where(row == 5, 1, jnp.where(row == 6, count - 2, count - 1))
    )
    weights = jnp.where(
        row < 4, jnp.where(slot < count, own, F32(0.0)), ones_where(slot == edge)
    ).astype(BF16)
    lane8, row8 = iota((8, 128), 1), iota((8, 128), 0)
    margin = jnp.where(
        lane8 < 2, wide[:, 0:128], pltpu.roll(wide[:, 256:384], 128 - (YR - 256), 1)
    )
    ys = column_tiles(pad_ref, 8)
    live = iota((YR, XW), 0) < count
    top = jnp.zeros((YR, XW), F32)
    for z in range(4):
        speed = jnp.abs(v_ref[z].astype(F32)) * xs_ref[...]
        speed = speed + jnp.abs(v_ref[4 + z].astype(F32)) * ys
        top = jnp.maximum(top, speed)
    top = jnp.where(live, top, F32(0.0))
    top = jnp.max(jnp.max(top, axis=0, keepdims=True), axis=1, keepdims=True)
    last = jnp.where(row8 < 4, margin, pltpu.roll(max_tile(top), 4, 0))
    for half in range(2):
        tiles = [nn(weights, v_ref[HALF * half + g]) for g in range(HALF)]
        whole = jnp.concatenate(tiles + [last], axis=0).astype(BF16)
        for chip in range(NROW // 2):
            o_ref[2 * chip + half] = whole


def x_solve_kernel(c_ref, x_ref, coupling_ref, o_ref, a_ref, e_ref, s_ref):
    a_ref[...] = c_ref[...].astype(F32).reshape(NCOL * 8, 128)
    part = [a_ref[pl.ds(v, NCOL, stride=8), :] for v in range(8)]
    margin = [pltpu.roll(part[6], 1, 0), pltpu.roll(part[7], 1, 0)]
    margin += [pltpu.roll(part[4], NCOL - 1, 0), pltpu.roll(part[5], NCOL - 1, 0)]
    local = x_ref[...].astype(F32)
    for k in range(2):
        for e in range(2):
            ends = part[2 * k + e]
            lane = (XW - 1) * e
            for h in range(4):
                place = 2 * HALO_X[h] + k
                ends = ends + local[place : place + 1, lane : lane + 1] * margin[h]
            e_ref[k, pl.ds(e, NCOL, stride=2), :] = ends
        s_ref[k] = nn(coupling_ref[k], e_ref[k], lax.Precision.HIGHEST)
        for e in range(2):
            a_ref[pl.ds(2 * k + e, NCOL, stride=8), :] = s_ref[k, pl.ds(e, NCOL, stride=2), :]
    for h in range(4):
        a_ref[pl.ds(4 + h, NCOL, stride=8), :] = margin[h]
    o_ref[...] = a_ref[...].reshape(NCOL, 8, 128).astype(BF16)


def top_kernel(s_ref, r_ref, o_ref):
    last = r_ref[...][:, 8 * HALF : 8 * TILES, :].astype(F32)
    row = iota((NROW, 8, 128), 1)
    parts = jnp.where((row >= 4) & (row < 7), last, F32(0.0))
    top = jnp.max(jnp.sum(parts, axis=1), axis=0, keepdims=True)
    spare = iota((8, 128), 1) >= CHUNK
    tile = max_tile(top)
    o_ref[...] = jnp.where(spare[None], tile[None], s_ref[...].astype(F32)).astype(BF16)


def y_solve_kernel(r_ref, coupling_ref, keep_ref, send_ref, a_ref, e_ref, s_ref, m_ref):
    a_ref[...] = r_ref[...].astype(F32).reshape(NROW * 8 * TILES, 128)

    def rows_of(place):
        return a_ref[pl.ds(place, NROW, stride=8 * TILES), :]

    source = iota((NROW, 128), 0)
    weights = [rows_of(8 * HALF + j) for j in range(4)]
    weight = [
        [jnp.broadcast_to(weights[j][:, h : h + 1], (NROW, 128)) for h in range(4)]
        for j in range(4)
    ]
    for g in range(HALF):
        lanes = slice(128 * g, 128 * g + 128)
        part = [rows_of(8 * g + v) for v in range(8)]
        margin = [pltpu.roll(part[6 + h], 1, 0) for h in range(2)]
        margin = [jnp.where(source == 0, F32(0.0), m) for m in margin]
        upper = [pltpu.roll(part[4 + h], NROW - 1, 0) for h in range(2)]
        margin += [jnp.where(source == NROW - 1, F32(0.0), m) for m in upper]
        for h in range(4):
            m_ref[h, :, lanes] = margin[h]
        for k in range(2):
            for e in range(2):
                ends = part[2 * k + e]
                for h in range(4):
                    ends = ends + weight[2 * k + e][h] * margin[h]
                e_ref[HALF * k + g, pl.ds(e, NROW, stride=2), :] = ends
    for k in range(2):
        ends = jnp.concatenate([e_ref[HALF * k + g] for g in range(HALF)], axis=1)
        s_ref[k] = nn(coupling_ref[k], ends, lax.Precision.HIGHEST)
    core = lax.axis_index("row_1")
    own = row_pos()
    for block, out in ((own, keep_ref), (own + 1 - 2 * core, send_ref)):
        pieces = [s_ref[k, pl.ds(2 * block + e, 1), :] for k in range(2) for e in range(2)]
        pieces += [m_ref[h, pl.ds(block, 1), :] for h in range(4)]
        out[...] = jnp.concatenate(pieces, axis=0).astype(BF16)


def prepare_kernel(
    count_ref, x_ref, xb_ref, w_ref, yb_ref, ys_ref, yc_ref,
    xo_ref, xc_ref, wm_ref, hc_ref, yy_ref, pad_ref,
):
    count = count_ref[row_pos()]
    x_all = x_ref[...]
    n_in = 2 * (XW + 4)
    dst, src = iota((XW, n_in), 0), iota((XW, n_in), 1)
    row, col = iota((8, n_in), 0), iota((8, n_in), 1)
    row_x, row_y = iota((8, XW), 0), iota((8, YR), 0)
    row_h, col_h = iota((8, YR + 4), 0), iota((8, YR + 4), 1)
    slot_in, slot_out = iota((YR + 4, YR), 0), iota((YR + 4, YR), 1)
    shift = ones_where((slot_in == slot_out + 2) & (slot_out < count)).astype(BF16)

    def placed(values, offsets):
        found = jnp.where(values[0] == 4, offsets[0], -1)
        for h in range(1, 4):
            found = jnp.where(values[0] == 4 + h, offsets[h], found)
        return ones_where(values[1] == found).astype(BF16)

    x_high = xb_ref[...].astype(BF16).astype(F32)
    y_high = yb_ref[...].astype(BF16).astype(F32)
    pick_y = placed((row_h, col_h), (0, 1, YR + 2, YR + 3))
    for k in range(2):
        lanes = slice(XW * k, XW * k + XW)
        xo_ref[:, lanes] = nn(ones_where(src == 2 * (dst + 2) + k).astype(BF16), x_all).astype(BF16)
        pick_x = placed((row, col), [2 * h + k for h in HALO_X])
        mine = (row_x // 2) == k
        head = jnp.where(mine, x_high, F32(0.0)) + nn(pick_x, x_all)
        tail = jnp.where(mine, xb_ref[...] - x_high, F32(0.0))
        xc_ref[:, lanes] = jnp.concatenate([head, tail], axis=0).astype(BF16)
        wm_ref[k] = nn(w_ref[k], shift).astype(BF16)
        mine = (row_y // 2) == k
        head = jnp.where(mine, y_high, F32(0.0)) + nt(pick_y, w_ref[k])
        tail = jnp.where(mine, yb_ref[...] - y_high, F32(0.0))
        hc_ref[k] = jnp.concatenate([head, tail], axis=0).astype(BF16)
    pad_ref[...] = jnp.zeros_like(pad_ref)
    pad_ref[0:1, 0:YR] = ys_ref[...]
    pad_ref[1:2, 0:YR] = yc_ref[...]
    scale = column_tiles(pad_ref, 0)
    yy_ref[0] = scale
    yy_ref[1] = viscosity * column_tiles(pad_ref, 1)
    yy_ref[2] = viscosity * scale * scale


def finish_kernel(
    count_ref, c_ref, keep_ref, got_ref, v_ref, p_ref, xs_ref, xv_ref,
    xo_ref, xc_ref, wm_ref, hc_ref, yy_ref, rhs_ref, inc_ref, x_add,
):
    count = count_ref[row_pos()]
    core = lax.axis_index("row_1")
    row, lane = iota((NCOL, 8, 128), 1), iota((NCOL, 8, 128), 2)
    tops = jnp.where((lane >= CHUNK) & (row < 3), c_ref[...].astype(F32), F32(0.0))
    top = jnp.max(jnp.sum(tops, axis=1), axis=0, keepdims=True)
    step = cfl_target / (jnp.max(top, axis=1, keepdims=True) + 1e-06)
    x_corr = xc_ref[...]
    for d in range(CHUNKS):
        coef = c_ref[d].astype(F32)
        coef = jnp.concatenate([coef, coef], axis=0).astype(BF16)
        x_add[CHUNK * d : CHUNK * d + 128, :] = tn(coef, x_corr)
    live = iota((YR, XW), 0) < count
    xs, xv = xs_ref[...], viscosity * xv_ref[...]
    x_second = viscosity * xs * xs
    for pair in range(2):
        for f in range(3):
            plane = 4 * f + 2 * pair
            half, g = divmod(plane, HALF)
            lanes = slice(128 * g, 128 * g + 256)
            coef = jnp.where(core == half, keep_ref[:, lanes].astype(F32), got_ref[:, lanes].astype(F32))
            coef = jnp.concatenate([coef, coef], axis=0).astype(BF16)
            both = jnp.concatenate([v_ref[plane], v_ref[plane + 1]], axis=1)
            y_first = nn(wm_ref[0], both) + tn(hc_ref[0], coef)
            y_second = nn(wm_ref[1], both) + tn(hc_ref[1], coef)
            for j in range(2):
                p, z = plane + j, 2 * pair + j
                at = slice(128 * j, 128 * j + 128)
                in_x = nn(v_ref[p], xo_ref[...]) + x_add[YR * p : YR * p + YR, :]
                u, v = v_ref[z].astype(F32), v_ref[4 + z].astype(F32)
                rhs = (xv - u * xs) * in_x[:, 0:XW] + x_second * in_x[:, XW:]
                rhs = rhs + (yy_ref[1] - v * yy_ref[0]) * y_first[:, at] + yy_ref[2] * y_second[:, at]
                rhs = jnp.where(live, rhs, F32(0.0))
                inc = step * (gamma_coef * rhs + zeta_coef * p_ref[p].astype(F32))
                inc = jnp.where(live, inc, F32(0.0))
                rhs_ref[p] = rhs.astype(BF16)
                inc_ref[p] = inc.astype(BF16)


VMEM = pl.BlockSpec(memory_space=pltpu.VMEM)
SMEM = pl.BlockSpec(memory_space=pltpu.SMEM)


def call(body, name, operands, outs, scratch=(), flops=0, mib=16):
    specs = [SMEM if operand.dtype == jnp.int32 else VMEM for operand in operands]
    size = sum(o.size * o.dtype.itemsize for o in (*operands, *outs))
    single = len(outs) == 1
    return pl.pallas_call(
        body,
        out_shape=outs[0] if single else outs,
        in_specs=specs,
        out_specs=VMEM if single else [VMEM] * len(outs),
        scratch_shapes=[pltpu.VMEM(shape, F32) for shape in scratch],
        compiler_params=pltpu.CompilerParams(vmem_limit_bytes=mib * 2**20),
        cost_estimate=pl.CostEstimate(flops=flops, bytes_accessed=size, transcendentals=0),
        name=name,
    )(*operands)


def shape(dims, kind=BF16):
    return jax.ShapeDtypeStruct(dims, kind)


def shards(
    velocity, rhs_prev, row_counts, x_scale, x_curv, y_scale, y_curv,
    x_local, x_coupling, x_basis, y_local, y_coupling, y_basis,
):
    lines = velocity.reshape(LINES, XW)
    planes = velocity.reshape(NP, YR, XW)
    previous = rhs_prev.reshape(NP, YR, XW)
    x_rows = x_local.reshape(2 * (XW + 4), XW)
    y_mats = jnp.transpose(y_local, (1, 2, 0))
    x_scale, x_curv = x_scale.reshape(1, XW), x_curv.reshape(1, XW)
    y_scale, y_curv = y_scale.reshape(1, YR), y_curv.reshape(1, YR)

    mine = call(x_partial_kernel, "x_partial", (lines, x_rows), (shape((NCOL, 8, 128)),), flops=10**8)
    theirs = lax.all_to_all(mine, COL, 0, 0, tiled=True)
    y_part = call(
        y_partial_kernel, "y_partial", (row_counts, planes, y_mats, x_scale, y_scale),
        (shape((NROW, 8 * TILES, 128)),), ((16, 384),), flops=10**8,
    )
    x_basis = jnp.pad(x_basis.reshape(4, XW), ((0, 4), (0, 0)))
    y_basis = jnp.pad(y_basis.reshape(4, YR), ((0, 4), (0, 0)))
    prepared = call(
        prepare_kernel, "prepare",
        (row_counts, x_rows, x_basis, y_mats, y_basis, y_scale, y_curv),
        (
            shape((XW, 2 * XW)), shape((16, 2 * XW)), shape((2, YR, YR)),
            shape((2, 16, YR)), shape((3, YR, XW), F32),
        ),
        ((8, 384),), flops=10**8,
    )
    columns = lax.all_to_all(y_part, ROW, 0, 0, tiled=True)
    x_solved = call(
        x_solve_kernel, "x_solve", (theirs, x_rows, x_coupling), (shape((NCOL, 8, 128)),),
        ((NCOL * 8, 128), (2, 2 * NCOL, 128), (2, 2 * NCOL, 128)), flops=10**8,
    )
    x_back = call(top_kernel, "top", (x_solved, columns), (shape((NCOL, 8, 128)),))
    x_back = lax.all_to_all(x_back, COL, 0, 0, tiled=True)
    wide = 128 * HALF
    keep, send = call(
        y_solve_kernel, "y_solve", (columns, y_coupling), (shape((8, wide)), shape((8, wide))),
        (
            (NROW * 8 * TILES, 128), (NP, 2 * NROW, 128), (2, 2 * NROW, wide), (4, NROW, wide),
        ), flops=10**8,
    )
    got = lax.ppermute(send, "row_1", [(0, 1), (1, 0)])
    rhs, inc = call(
        finish_kernel, "finish",
        (row_counts, x_back, keep, got, planes, previous, x_scale, x_curv, *prepared),
        (shape((NP, YR, XW)), shape((NP, YR, XW))),
        ((CHUNK * (CHUNKS - 1) + 128, 2 * XW),), flops=6 * 10**8, mib=32,
    )
    return rhs.reshape(velocity.shape), inc.reshape(velocity.shape)


def solution(mesh):
    torus = Mesh(mesh.devices.reshape(8, 2, 8, 4), ("row_0", "row_1", "col_0", "col_1"))
    placed = (
        P(None, None, ROW, COL), P(None, None, ROW, COL), P(), P(COL), P(COL), P(ROW), P(ROW),
        P(), P(), P(), P(ROW, None, None), P(), P(ROW, None, None, None),
    )
    return jax.shard_map(
        shards,
        mesh=torus,
        in_specs=placed,
        out_specs=(P(None, None, ROW, COL), P(None, None, ROW, COL)),
        check_vma=False,
    )
```

```python
import jax
import jax.numpy as jnp
from jax import lax
from jax.experimental import pallas as pl
from jax.experimental.pallas import tpu as pltpu
from jax.sharding import Mesh
from jax.sharding import PartitionSpec as P

COL = ("col_0", "col_1")
ROW = ("row_0", "row_1")

viscosity = 0.1
cfl_target = 1.5
gamma_coef = 5.0 / 12.0
zeta_coef = -17.0 / 60.0

F32 = jnp.float32
BF16 = jnp.bfloat16
NCOL = 32
NROW = 16
XW = 128
YR = 264
NP = 12
LINES = NP * YR
CHUNK = 112
CHUNKS = -(-LINES // CHUNK)
HALF = NP // 2
TILES = HALF + 1
PIECE = 4 * CHUNK
PIECES = -(-(LINES - PIECE) // PIECE)
EDGE_X = (0, 1, XW - 2, XW - 1)
HALO_X = (0, 1, XW + 2, XW + 3)


def nn(a, b, precision=None):
    return lax.dot_general(
        a, b, (((1,), (0,)), ((), ())), precision=precision, preferred_element_type=F32
    )


def nt(a, b):
    return lax.dot_general(a, b, (((1,), (1,)), ((), ())), preferred_element_type=F32)


def tn(a, b):
    return lax.dot_general(a, b, (((0,), (0,)), ((), ())), preferred_element_type=F32)


def iota(shape, dim):
    return lax.broadcasted_iota(jnp.int32, shape, dim)


def ones_where(cond):
    return jnp.where(cond, F32(1.0), F32(0.0))


def row_pos():
    return lax.axis_index("row_0") * 2 + lax.axis_index("row_1")


def three_parts(value):
    high = value.astype(BF16).astype(F32)
    rest = value - high
    mid = rest.astype(BF16).astype(F32)
    return high, mid, rest - mid


def max_tile(value):
    high, mid, low = three_parts(jnp.broadcast_to(value, (8, 128)))
    row = iota((8, 128), 0)
    return jnp.where(
        row == 0, high, jnp.where(row == 1, mid, jnp.where(row == 2, low, F32(0.0)))
    )


def column_tiles(row_ref, row):
    pieces = []
    for j in range(3):
        seg = row_ref[row : row + 1, 128 * j : 128 * j + 128]
        pieces.append(jnp.transpose(jnp.broadcast_to(seg, (128, 128))))
    return jnp.concatenate([pieces[0], pieces[1], pieces[2][0 : YR - 256]], axis=0)


def x_partial_kernel(
    v_hbm, x_hbm, w_hbm, xs_hbm, ys_hbm, count_hbm,
    o_ref, v_ref, x_ref, w_ref, xs_ref, ys_ref, count_ref, counts, sems,
):
    copies = [pltpu.make_async_copy(x_hbm, x_ref, sems.at[0])]
    starts = list(range(0, LINES - PIECE, PIECE)) + [LINES]
    starts[-2:] = [starts[-2], LINES]
    for j in range(len(starts) - 1):
        rows = pl.ds(starts[j], starts[j + 1] - starts[j])
        copies.append(pltpu.make_async_copy(v_hbm.at[rows, :], v_ref.at[rows, :], sems.at[j + 1]))
    later = ((w_hbm, w_ref), (xs_hbm, xs_ref), (ys_hbm, ys_ref), (count_hbm, counts))
    later = [pltpu.make_async_copy(*pair, sems.at[len(starts) + j]) for j, pair in enumerate(later)]
    for copy in copies + later:
        copy.start()
    row, lane = iota((8, XW), 0), iota((8, XW), 1)
    pick = ones_where((row < 4) & (lane == (XW - 1) * (row % 2))).astype(BF16)
    row_e = iota((8, 2 * (XW + 4)), 0)
    edges = jnp.where(row == 4, ones_where(lane == EDGE_X[0]), F32(0.0))
    for j in range(1, 4):
        edges = jnp.where(row == 4 + j, ones_where(lane == EDGE_X[j]), edges)
    src, dst = iota((2 * (XW + 4), XW), 0), iota((2 * (XW + 4), XW), 1)
    spread = ones_where(src // 2 == dst + 2).astype(BF16)
    mine = iota((8, 2 * (XW + 4)), 1) % 2 == row_e // 2
    copies[0].wait()
    ends = jnp.where(mine, nt(pick, x_ref[...]), F32(0.0)).astype(BF16)
    weights = (edges + nn(ends, spread)).astype(BF16)
    arrived = 0
    for d in range(NCOL):
        first = CHUNK * d
        last = min(first + 128, LINES)
        while arrived < len(starts) - 1 and starts[arrived] < last:
            arrived += 1
            copies[arrived].wait()
        if first + 128 <= LINES:
            o_ref[d] = nt(weights, v_ref[first : first + 128, :]).astype(BF16)
        elif first < LINES:
            part = nt(weights, v_ref[first:LINES, :])
            rest = jnp.zeros((8, 128 - (LINES - first)), F32)
            o_ref[d] = jnp.concatenate([part, rest], axis=1).astype(BF16)
        else:
            o_ref[d] = jnp.zeros((8, 128), BF16)
    for copy in later:
        copy.wait()
    count_ref[...] = jnp.full((8, 128), counts[row_pos()], jnp.int32)


def y_partial_kernel(count_ref, v_ref, w_ref, xs_ref, ys_ref, o_ref, pad_ref):
    count = count_ref[0:1, 0:1]
    row, slot = iota((8, YR), 0), iota((8, YR), 1)
    place = jnp.where(row % 2 == 0, 0, count - 1)
    ends = nn(ones_where((row < 2) & (slot == place)).astype(BF16), w_ref[0])
    ends = ends + nn(
        ones_where((row >= 2) & (row < 4) & (slot == place)).astype(BF16), w_ref[1]
    )
    pad_ref[...] = jnp.zeros_like(pad_ref)
    pad_ref[0:8, 0 : YR + 4] = ends
    pad_ref[8:9, 0:YR] = ys_ref[...].reshape(1, YR)
    wide = pad_ref[0:8, :]
    own = pltpu.roll(wide, 384 - 2, 1)[:, 0:YR]
    edge = jnp.where(
        row == 4, 0, jnp.where(row == 5, 1, jnp.where(row == 6, count - 2, count - 1))
    )
    weights = jnp.where(
        row < 4, jnp.where(slot < count, own, F32(0.0)), ones_where(slot == edge)
    ).astype(BF16)
    lane8, row8 = iota((8, 128), 1), iota((8, 128), 0)
    margin = jnp.where(
        lane8 < 2, wide[:, 0:128], pltpu.roll(wide[:, 256:384], 128 - (YR - 256), 1)
    )
    ys = column_tiles(pad_ref, 8)
    live = iota((YR, XW), 0) < count
    top = jnp.zeros((YR, XW), F32)
    for z in range(4):
        speed = jnp.abs(v_ref[z].astype(F32)) * xs_ref[...]
        speed = speed + jnp.abs(v_ref[4 + z].astype(F32)) * ys
        top = jnp.maximum(top, speed)
    top = jnp.where(live, top, F32(0.0))
    top = jnp.max(jnp.max(top, axis=0, keepdims=True), axis=1, keepdims=True)
    last = jnp.where(row8 < 4, margin, pltpu.roll(max_tile(top), 4, 0))
    for half in range(2):
        tiles = [nn(weights, v_ref[HALF * half + g]) for g in range(HALF)]
        whole = jnp.concatenate(tiles + [last], axis=0).astype(BF16)
        for chip in range(NROW // 2):
            o_ref[2 * chip + half] = whole


def x_solve_kernel(c_ref, x_ref, coupling_ref, o_ref, a_ref, e_ref, s_ref):
    a_ref[...] = c_ref[...].astype(F32).reshape(NCOL * 8, 128)
    part = [a_ref[pl.ds(v, NCOL, stride=8), :] for v in range(8)]
    margin = [pltpu.roll(part[6], 1, 0), pltpu.roll(part[7], 1, 0)]
    margin += [pltpu.roll(part[4], NCOL - 1, 0), pltpu.roll(part[5], NCOL - 1, 0)]
    local = x_ref[...].astype(F32)
    for k in range(2):
        for e in range(2):
            ends = part[2 * k + e]
            lane = (XW - 1) * e
            for h in range(4):
                place = 2 * HALO_X[h] + k
                ends = ends + local[place : place + 1, lane : lane + 1] * margin[h]
            e_ref[k, pl.ds(e, NCOL, stride=2), :] = ends
        s_ref[k] = nn(coupling_ref[k], e_ref[k], lax.Precision.HIGHEST)
        for e in range(2):
            a_ref[pl.ds(2 * k + e, NCOL, stride=8), :] = s_ref[k, pl.ds(e, NCOL, stride=2), :]
    for h in range(4):
        a_ref[pl.ds(4 + h, NCOL, stride=8), :] = margin[h]
    o_ref[...] = a_ref[...].reshape(NCOL, 8, 128).astype(BF16)


def top_of(ref, first, count, stride):
    parts = [ref[pl.ds(first + j, count, stride=stride), :] for j in range(3)]
    return jnp.max(parts[0] + parts[1] + parts[2], axis=0, keepdims=True)


def top_kernel(s_ref, r_ref, after_ref, o_ref, t_ref):
    t_ref[...] = r_ref[...][:, 8 * HALF : 8 * TILES, :].astype(F32).reshape(8 * NROW, 128)
    tile = max_tile(top_of(t_ref, 4, NROW, 8))
    spare = iota((8, 128), 1) >= CHUNK
    o_ref[...] = jnp.where(spare[None], tile[None], s_ref[...].astype(F32)).astype(BF16)


def y_solve_kernel(r_ref, coupling_ref, keep_ref, send_ref, a_ref, e_ref, s_ref, m_ref):
    a_ref[...] = r_ref[...].astype(F32).reshape(NROW * 8 * TILES, 128)

    def rows_of(place):
        return a_ref[pl.ds(place, NROW, stride=8 * TILES), :]

    source = iota((NROW, 128), 0)
    weights = [rows_of(8 * HALF + j) for j in range(4)]
    weight = [
        [jnp.broadcast_to(weights[j][:, h : h + 1], (NROW, 128)) for h in range(4)]
        for j in range(4)
    ]
    for g in range(HALF):
        lanes = slice(128 * g, 128 * g + 128)
        part = [rows_of(8 * g + v) for v in range(8)]
        margin = [pltpu.roll(part[6 + h], 1, 0) for h in range(2)]
        margin = [jnp.where(source == 0, F32(0.0), m) for m in margin]
        upper = [pltpu.roll(part[4 + h], NROW - 1, 0) for h in range(2)]
        margin += [jnp.where(source == NROW - 1, F32(0.0), m) for m in upper]
        for h in range(4):
            m_ref[h, :, lanes] = margin[h]
        for k in range(2):
            for e in range(2):
                ends = part[2 * k + e]
                for h in range(4):
                    ends = ends + weight[2 * k + e][h] * margin[h]
                e_ref[HALF * k + g, pl.ds(e, NROW, stride=2), :] = ends
    for k in range(2):
        ends = jnp.concatenate([e_ref[HALF * k + g] for g in range(HALF)], axis=1)
        s_ref[k] = nn(coupling_ref[k], ends, lax.Precision.HIGHEST)
    core = lax.axis_index("row_1")
    own = row_pos()
    for block, out in ((own, keep_ref), (own + 1 - 2 * core, send_ref)):
        pieces = [s_ref[k, pl.ds(2 * block + e, 1), :] for k in range(2) for e in range(2)]
        pieces += [m_ref[h, pl.ds(block, 1), :] for h in range(4)]
        out[...] = jnp.concatenate(pieces, axis=0).astype(BF16)


def own_kernel(
    count_ref, v_ref, x_ref, xb_ref, w_ref, yb_ref, xs_ref, xv_ref, ys_ref, yc_ref,
    after_ref, own_ref, xc_ref, hc_ref, xx_ref, yy_ref, xo_ref, wm_ref,
):
    count = count_ref[0:1, 0:1]
    x_all = x_ref[...]
    n_in = 2 * (XW + 4)
    dst, src = iota((XW, n_in), 0), iota((XW, n_in), 1)
    row, col = iota((8, n_in), 0), iota((8, n_in), 1)
    row_x, row_y = iota((8, XW), 0), iota((8, YR), 0)
    row_h, col_h = iota((8, YR + 4), 0), iota((8, YR + 4), 1)
    slot_in, slot_out = iota((YR + 4, YR), 0), iota((YR + 4, YR), 1)
    shift = ones_where((slot_in == slot_out + 2) & (slot_out < count)).astype(BF16)

    def placed(values, offsets):
        found = jnp.where(values[0] == 4, offsets[0], -1)
        for h in range(1, 4):
            found = jnp.where(values[0] == 4 + h, offsets[h], found)
        return ones_where(values[1] == found).astype(BF16)

    x_high = xb_ref[...].astype(BF16).astype(F32)
    y_high = yb_ref[...].astype(BF16).astype(F32)
    pick_y = placed((row_h, col_h), (0, 1, YR + 2, YR + 3))
    for k in range(2):
        lanes = slice(XW * k, XW * k + XW)
        xo_ref[:, lanes] = nn(ones_where(src == 2 * (dst + 2) + k).astype(BF16), x_all).astype(BF16)
        pick_x = placed((row, col), [2 * h + k for h in HALO_X])
        mine = (row_x // 2) == k
        head = jnp.where(mine, x_high, F32(0.0)) + nn(pick_x, x_all)
        tail = jnp.where(mine, xb_ref[...] - x_high, F32(0.0))
        xc_ref[:, lanes] = jnp.concatenate([head, tail], axis=0).astype(BF16)
        wm_ref[k] = nn(w_ref[k], shift).astype(BF16)
        mine = (row_y // 2) == k
        head = jnp.where(mine, y_high, F32(0.0)) + nt(pick_y, w_ref[k])
        tail = jnp.where(mine, yb_ref[...] - y_high, F32(0.0))
        hc_ref[k] = jnp.concatenate([head, tail], axis=0).astype(BF16)
    yy_ref[...] = jnp.zeros_like(yy_ref)
    ys = ys_ref[...].reshape(1, YR)
    yy_ref[0:1, 0:YR] = ys
    yy_ref[1:2, 0:YR] = viscosity * yc_ref[...].reshape(1, YR)
    yy_ref[2:3, 0:YR] = viscosity * ys * ys
    scale, curv, y_second = (column_tiles(yy_ref, j) for j in range(3))
    xs, xv = xs_ref[...], viscosity * xv_ref[...]
    x_second = viscosity * xs * xs
    xx_ref[...] = jnp.concatenate([xs, xv, x_second, jnp.zeros((5, XW), F32)], axis=0)
    for pair in range(2):
        for f in range(3):
            plane = 4 * f + 2 * pair
            both = jnp.concatenate([v_ref[plane], v_ref[plane + 1]], axis=1)
            of_first, of_second = nn(wm_ref[0], both), nn(wm_ref[1], both)
            for j in range(2):
                p, z = plane + j, 2 * pair + j
                at = slice(XW * j, XW * j + XW)
                in_x = nn(v_ref[p], xo_ref[...])
                u, v = v_ref[z].astype(F32), v_ref[4 + z].astype(F32)
                rhs = (xv - u * xs) * in_x[:, 0:XW] + x_second * in_x[:, XW:]
                rhs = rhs + (curv - v * scale) * of_first[:, at]
                own_ref[p] = rhs + y_second * of_second[:, at]


def y_add_kernel(keep_ref, got_ref, v_ref, own_ref, hc_ref, yy_ref, o_ref):
    scale, curv, y_second = (column_tiles(yy_ref, j) for j in range(3))
    core = lax.axis_index("row_1")
    for pair in range(2):
        for f in range(3):
            plane = 4 * f + 2 * pair
            half, g = divmod(plane, HALF)
            lanes = slice(128 * g, 128 * g + 256)
            coef = jnp.where(core == half, keep_ref[:, lanes].astype(F32), got_ref[:, lanes].astype(F32))
            coef = jnp.concatenate([coef, coef], axis=0).astype(BF16)
            of_first, of_second = tn(hc_ref[0], coef), tn(hc_ref[1], coef)
            for j in range(2):
                p, z = plane + j, 2 * pair + j
                at = slice(XW * j, XW * j + XW)
                v = v_ref[4 + z].astype(F32)
                add = (curv - v * scale) * of_first[:, at] + y_second * of_second[:, at]
                o_ref[p] = own_ref[p] + add


def finish_kernel(
    count_ref, c_ref, v_ref, p_ref, base_ref, xc_ref, xx_ref, rhs_hbm, inc_hbm,
    x_add, t_ref, rhs_ref, inc_ref, sems,
):
    count = count_ref[0:1, 0:1]
    t_ref[...] = c_ref[...].astype(F32).reshape(8 * NCOL, 128)
    top = top_of(t_ref, 0, NCOL, 8)
    spare = iota((1, 128), 1) >= CHUNK
    top = jnp.max(jnp.where(spare, top, F32(0.0)), axis=1, keepdims=True)
    step = cfl_target / (top + 1e-06)
    x_corr = xc_ref[...]
    live = iota((YR, XW), 0) < count
    xs, xv, x_second = xx_ref[0:1, :], xx_ref[1:2, :], xx_ref[2:3, :]
    done, copies = 0, []
    for p in range(NP):
        while done < CHUNKS and CHUNK * done < YR * (p + 1):
            coef = t_ref[8 * done : 8 * done + 8, :]
            coef = jnp.concatenate([coef, coef], axis=0).astype(BF16)
            x_add[CHUNK * done : CHUNK * done + 128, :] = tn(coef, x_corr)
            done += 1
        u = v_ref[p % 4].astype(F32)
        add = x_add[YR * p : YR * p + YR, :]
        rhs = base_ref[p] + (xv - u * xs) * add[:, 0:XW] + x_second * add[:, XW:]
        rhs = jnp.where(live, rhs, F32(0.0))
        inc = step * (gamma_coef * rhs + zeta_coef * p_ref[p].astype(F32))
        rhs_ref[p] = rhs.astype(BF16)
        inc_ref[p] = jnp.where(live, inc, F32(0.0)).astype(BF16)
        for j, (source, target) in enumerate(((rhs_ref, rhs_hbm), (inc_ref, inc_hbm))):
            copies.append(pltpu.make_async_copy(source.at[p], target.at[p], sems.at[j, p]))
            copies[-1].start()
    for copy in copies:
        copy.wait()


VMEM = pl.BlockSpec(memory_space=pltpu.VMEM)
HBM = pl.BlockSpec(memory_space=pltpu.HBM)


def call(body, name, operands, outs, scratch=(), flops=0, mib=6, far=(), far_out=False, alias=None):
    specs = [HBM if j in far else VMEM for j in range(len(operands))]
    size = sum(o.size * o.dtype.itemsize for o in operands)
    single = len(outs) == 1
    out_spec = HBM if far_out else VMEM
    return pl.pallas_call(
        body,
        out_shape=outs[0] if single else outs,
        in_specs=specs,
        out_specs=out_spec if single else [out_spec] * len(outs),
        scratch_shapes=[pltpu.VMEM(item, F32) if isinstance(item, tuple) else item for item in scratch],
        compiler_params=pltpu.CompilerParams(vmem_limit_bytes=mib * 2**20),
        cost_estimate=pl.CostEstimate(flops=flops, bytes_accessed=size, transcendentals=0),
        input_output_aliases=alias or {},
        name=name,
    )(*operands)


def shape(dims, kind=BF16):
    return jax.ShapeDtypeStruct(dims, kind)


def shards(
    velocity, rhs_prev, row_counts, x_scale, x_curv, y_scale, y_curv,
    x_local, x_coupling, x_basis, y_local, y_coupling, y_basis,
):
    lines = velocity.reshape(LINES, XW)
    previous = rhs_prev.reshape(NP, YR, XW)
    x_rows = x_local.reshape(2 * (XW + 4), XW)
    y_mats = jnp.transpose(y_local, (1, 2, 0))
    x_scale, x_curv = x_scale.reshape(1, XW), x_curv.reshape(1, XW)

    fetched = (lines, x_rows, y_mats, x_scale, y_scale)
    *fetched, row_counts = [
        pltpu.with_memory_space_constraint(item, pltpu.HBM) for item in (*fetched, row_counts)
    ]
    mine, lines, x_rows, y_mats, x_scale, y_scale, count = call(
        x_partial_kernel, "x_partial", (*fetched, row_counts),
        (
            shape((NCOL, 8, 128)), *(pltpu.VMEM(item.shape, item.dtype) for item in fetched),
            pltpu.VMEM((8, 128), jnp.int32),
        ),
        (pltpu.SMEM((NROW,), jnp.int32), pltpu.SemaphoreType.DMA((PIECES + 5,))),
        flops=10**8, far=range(6),
    )
    planes = lines.reshape(NP, YR, XW)
    theirs = lax.all_to_all(mine, COL, 0, 0, tiled=True)
    y_part = call(
        y_partial_kernel, "y_partial", (count, planes, y_mats, x_scale, y_scale),
        (shape((NROW, 8 * TILES, 128)),), ((16, 384),), flops=10**8,
    )
    x_basis = jnp.pad(x_basis.reshape(4, XW), ((0, 4), (0, 0)))
    y_basis = jnp.pad(y_basis.reshape(4, YR), ((0, 4), (0, 0)))
    columns = lax.all_to_all(y_part, ROW, 0, 0, tiled=True)
    x_solved = call(
        x_solve_kernel, "x_solve", (theirs, x_rows, x_coupling), (shape((NCOL, 8, 128)),),
        ((NCOL * 8, 128), (2, 2 * NCOL, 128), (2, 2 * NCOL, 128)), flops=10**8,
    )
    own, x_corr, y_corr, x_lines, y_lines = call(
        own_kernel, "own",
        (count, planes, x_rows, x_basis, y_mats, y_basis, x_scale, x_curv, y_scale, y_curv,
            y_part),
        (
            shape((NP, YR, XW), F32), shape((16, 2 * XW)), shape((2, 16, YR)),
            shape((8, XW), F32), shape((8, 384), F32),
        ),
        (pltpu.VMEM((XW, 2 * XW), BF16), pltpu.VMEM((2, YR, YR), BF16)),
        flops=6 * 10**8, mib=8, far=(10,),
    )
    x_back = call(
        top_kernel, "top", (x_solved, columns, x_lines), (shape((NCOL, 8, 128)),),
        ((8 * NROW, 128),), far=(2,),
    )
    x_back = lax.all_to_all(x_back, COL, 0, 0, tiled=True)
    wide = 128 * HALF
    keep, send = call(
        y_solve_kernel, "y_solve", (columns, y_coupling), (shape((8, wide)), shape((8, wide))),
        (
            (NROW * 8 * TILES, 128), (NP, 2 * NROW, 128), (2, 2 * NROW, wide), (4, NROW, wide),
        ), flops=10**8,
    )
    got = lax.ppermute(send, "row_1", [(0, 1), (1, 0)])
    base = call(
        y_add_kernel, "y_add", (keep, got, planes, own, y_corr, y_lines),
        (shape(own.shape, F32),), flops=10**8, alias={3: 0},
    )
    rhs, inc = call(
        finish_kernel, "finish",
        (count, x_back, planes, previous, base, x_corr, x_lines),
        (shape((NP, YR, XW)), shape((NP, YR, XW))),
        (
            (CHUNK * (CHUNKS - 1) + 128, 2 * XW), (8 * NCOL, 128),
            pltpu.VMEM((NP, YR, XW), BF16), pltpu.VMEM((NP, YR, XW), BF16),
            pltpu.SemaphoreType.DMA((2, NP)),
        ), flops=10**8, mib=10, far_out=True,
    )
    return rhs.reshape(velocity.shape), inc.reshape(velocity.shape)


def solution(mesh):
    torus = Mesh(mesh.devices.reshape(8, 2, 8, 4), ("row_0", "row_1", "col_0", "col_1"))
    placed = (
        P(None, None, ROW, COL), P(None, None, ROW, COL), P(), P(COL), P(COL), P(ROW), P(ROW),
        P(), P(), P(), P(ROW, None, None), P(), P(ROW, None, None, None),
    )
    return jax.shard_map(
        shards,
        mesh=torus,
        in_specs=placed,
        out_specs=(P(None, None, ROW, COL), P(None, None, ROW, COL)),
        check_vma=False,
    )
```

```python
import functools

import jax
import jax.numpy as jnp
from jax import lax
from jax.experimental import pallas as pl
from jax.experimental.pallas import tpu as pltpu
from jax.sharding import Mesh
from jax.sharding import PartitionSpec as P

COL = ("col_0", "col_1")
ROW = ("row_0", "row_1")

viscosity = 0.1
cfl_target = 1.5
gamma_coef = 5.0 / 12.0
zeta_coef = -17.0 / 60.0

F32 = jnp.float32
BF16 = jnp.bfloat16
NCOL = 32
NROW = 16
XW = 128
YR = 264
NP = 12
LINES = NP * YR
CHUNK = 112
CHUNKS = -(-LINES // CHUNK)
HALF = NP // 2
TILES = HALF + 1
GROUP = 4
EDGE_X = (0, 1, XW - 2, XW - 1)
HALO_X = (0, 1, XW + 2, XW + 3)


def nn(a, b, precision=None):
    return lax.dot_general(
        a, b, (((1,), (0,)), ((), ())), precision=precision, preferred_element_type=F32
    )


def nt(a, b):
    return lax.dot_general(a, b, (((1,), (1,)), ((), ())), preferred_element_type=F32)


def tn(a, b):
    return lax.dot_general(a, b, (((0,), (0,)), ((), ())), preferred_element_type=F32)


def iota(shape, dim):
    return lax.broadcasted_iota(jnp.int32, shape, dim)


def ones_where(cond):
    return jnp.where(cond, F32(1.0), F32(0.0))


def row_pos():
    return lax.axis_index("row_0") * 2 + lax.axis_index("row_1")


def three_parts(value):
    high = value.astype(BF16).astype(F32)
    rest = value - high
    mid = rest.astype(BF16).astype(F32)
    return high, mid, rest - mid


def max_tile(value):
    high, mid, low = three_parts(jnp.broadcast_to(value, (8, 128)))
    row = iota((8, 128), 0)
    return jnp.where(
        row == 0, high, jnp.where(row == 1, mid, jnp.where(row == 2, low, F32(0.0)))
    )


def column_tiles(row_ref, row):
    pieces = []
    for j in range(3):
        seg = row_ref[row : row + 1, 128 * j : 128 * j + 128]
        pieces.append(jnp.transpose(jnp.broadcast_to(seg, (128, 128))))
    return jnp.concatenate([pieces[0], pieces[1], pieces[2][0 : YR - 256]], axis=0)


def x_partial_kernel(
    v_hbm, x_hbm, w_hbm, xs_hbm, ys_hbm, count_hbm,
    o_ref, v_ref, x_ref, w_ref, xs_ref, ys_ref, count_ref, counts, sems,
):
    copies = [
        pltpu.make_async_copy(x_hbm, x_ref, sems.at[0]), pltpu.make_async_copy(v_hbm, v_ref, sems.at[1])
    ]
    later = ((w_hbm, w_ref), (xs_hbm, xs_ref), (ys_hbm, ys_ref), (count_hbm, counts))
    later = [pltpu.make_async_copy(*pair, sems.at[2 + j]) for j, pair in enumerate(later)]
    for copy in copies + later:
        copy.start()
    row, lane = iota((8, XW), 0), iota((8, XW), 1)
    pick = ones_where((row < 4) & (lane == (XW - 1) * (row % 2))).astype(BF16)
    row_e = iota((8, 2 * (XW + 4)), 0)
    edges = jnp.where(row == 4, ones_where(lane == EDGE_X[0]), F32(0.0))
    for j in range(1, 4):
        edges = jnp.where(row == 4 + j, ones_where(lane == EDGE_X[j]), edges)
    src, dst = iota((2 * (XW + 4), XW), 0), iota((2 * (XW + 4), XW), 1)
    spread = ones_where(src // 2 == dst + 2).astype(BF16)
    mine = iota((8, 2 * (XW + 4)), 1) % 2 == row_e // 2
    copies[0].wait()
    ends = jnp.where(mine, nt(pick, x_ref[...]), F32(0.0)).astype(BF16)
    weights = (edges + nn(ends, spread)).astype(BF16)
    o_ref[CHUNKS:] = jnp.zeros((NCOL - CHUNKS, 8, 128), BF16)
    copies[1].wait()
    for d in range(0, NCOL, 2):
        first = CHUNK * d
        last = min(first + 256, LINES)
        if last - first == 256:
            pair = nt(weights, v_ref[first:last, :])
            o_ref[d] = pair[:, 0:128].astype(BF16)
            o_ref[d + 1] = pltpu.roll(pair, 256 - CHUNK, 1)[:, 0:128].astype(BF16)
        elif last > first:
            part = nt(weights, v_ref[first:last, :])
            rest = jnp.zeros((8, 128 - (last - first)), F32)
            o_ref[d] = jnp.concatenate([part, rest], axis=1).astype(BF16)
    for copy in later:
        copy.wait()
    count_ref[...] = jnp.full((8, 128), counts[row_pos()], jnp.int32)


def y_partial_kernel(count_ref, v_ref, w_ref, xs_ref, ys_ref, o_ref, pad_ref):
    count = count_ref[0:1, 0:1]
    row, slot = iota((8, YR), 0), iota((8, YR), 1)
    place = jnp.where(row % 2 == 0, 0, count - 1)
    ends = nn(ones_where((row < 2) & (slot == place)).astype(BF16), w_ref[0])
    ends = ends + nn(
        ones_where((row >= 2) & (row < 4) & (slot == place)).astype(BF16), w_ref[1]
    )
    pad_ref[...] = jnp.zeros_like(pad_ref)
    pad_ref[0:8, 0 : YR + 4] = ends
    pad_ref[8:9, 0:YR] = ys_ref[...].reshape(1, YR)
    wide = pad_ref[0:8, :]
    own = pltpu.roll(wide, 384 - 2, 1)[:, 0:YR]
    edge = jnp.where(
        row == 4, 0, jnp.where(row == 5, 1, jnp.where(row == 6, count - 2, count - 1))
    )
    weights = jnp.where(
        row < 4, jnp.where(slot < count, own, F32(0.0)), ones_where(slot == edge)
    ).astype(BF16)
    lane8, row8 = iota((8, 128), 1), iota((8, 128), 0)
    margin = jnp.where(
        lane8 < 2, wide[:, 0:128], pltpu.roll(wide[:, 256:384], 128 - (YR - 256), 1)
    )
    ys = column_tiles(pad_ref, 8)
    live = iota((YR, XW), 0) < count
    top = jnp.zeros((YR, XW), F32)
    for z in range(4):
        speed = jnp.abs(v_ref[z].astype(F32)) * xs_ref[...]
        speed = speed + jnp.abs(v_ref[4 + z].astype(F32)) * ys
        top = jnp.maximum(top, speed)
    top = jnp.where(live, top, F32(0.0))
    top = jnp.max(jnp.max(top, axis=0, keepdims=True), axis=1, keepdims=True)
    last = jnp.where(row8 < 4, margin, pltpu.roll(max_tile(top), 4, 0))
    for half in range(2):
        tiles = [nn(weights, v_ref[HALF * half + g]) for g in range(HALF)]
        whole = jnp.concatenate(tiles + [last], axis=0).astype(BF16)
        for chip in range(NROW // 2):
            o_ref[2 * chip + half] = whole


def x_solve_kernel(c_ref, x_ref, coupling_ref, o_ref, a_ref, e_ref, s_ref):
    a_ref[...] = c_ref[...].astype(F32).reshape(NCOL * 8, 128)
    part = [a_ref[pl.ds(v, NCOL, stride=8), :] for v in range(8)]
    margin = [pltpu.roll(part[6], 1, 0), pltpu.roll(part[7], 1, 0)]
    margin += [pltpu.roll(part[4], NCOL - 1, 0), pltpu.roll(part[5], NCOL - 1, 0)]
    local = x_ref[...].astype(F32)
    for k in range(2):
        for e in range(2):
            ends = part[2 * k + e]
            lane = (XW - 1) * e
            for h in range(4):
                place = 2 * HALO_X[h] + k
                ends = ends + local[place : place + 1, lane : lane + 1] * margin[h]
            e_ref[k, pl.ds(e, NCOL, stride=2), :] = ends
        s_ref[k] = nn(coupling_ref[k], e_ref[k], lax.Precision.HIGHEST)
        for e in range(2):
            a_ref[pl.ds(2 * k + e, NCOL, stride=8), :] = s_ref[k, pl.ds(e, NCOL, stride=2), :]
    for h in range(4):
        a_ref[pl.ds(4 + h, NCOL, stride=8), :] = margin[h]
    o_ref[...] = a_ref[...].reshape(NCOL, 8, 128).astype(BF16)


def top_of(ref, first, count, stride):
    parts = [ref[pl.ds(first + j, count, stride=stride), :] for j in range(3)]
    return jnp.max(parts[0] + parts[1] + parts[2], axis=0, keepdims=True)


def top_kernel(s_ref, r_ref, after_ref, o_ref, t_ref):
    t_ref[...] = r_ref[...][:, 8 * HALF : 8 * TILES, :].astype(F32).reshape(8 * NROW, 128)
    tile = max_tile(top_of(t_ref, 4, NROW, 8))
    spare = iota((8, 128), 1) >= CHUNK
    o_ref[...] = jnp.where(spare[None], tile[None], s_ref[...].astype(F32)).astype(BF16)


def y_solve_kernel(r_ref, coupling_ref, keep_ref, send_ref, a_ref, e_ref, s_ref, m_ref):
    a_ref[...] = r_ref[...].astype(F32).reshape(NROW * 8 * TILES, 128)

    def rows_of(place):
        return a_ref[pl.ds(place, NROW, stride=8 * TILES), :]

    source = iota((NROW, 128), 0)
    weights = [rows_of(8 * HALF + j) for j in range(4)]
    weight = [
        [jnp.broadcast_to(weights[j][:, h : h + 1], (NROW, 128)) for h in range(4)]
        for j in range(4)
    ]
    for g in range(HALF):
        lanes = slice(128 * g, 128 * g + 128)
        part = [rows_of(8 * g + v) for v in range(8)]
        margin = [pltpu.roll(part[6 + h], 1, 0) for h in range(2)]
        margin = [jnp.where(source == 0, F32(0.0), m) for m in margin]
        upper = [pltpu.roll(part[4 + h], NROW - 1, 0) for h in range(2)]
        margin += [jnp.where(source == NROW - 1, F32(0.0), m) for m in upper]
        for h in range(4):
            m_ref[h, :, lanes] = margin[h]
        for k in range(2):
            for e in range(2):
                ends = part[2 * k + e]
                for h in range(4):
                    ends = ends + weight[2 * k + e][h] * margin[h]
                e_ref[HALF * k + g, pl.ds(e, NROW, stride=2), :] = ends
    for k in range(2):
        ends = jnp.concatenate([e_ref[HALF * k + g] for g in range(HALF)], axis=1)
        s_ref[k] = nn(coupling_ref[k], ends, lax.Precision.HIGHEST)
    core = lax.axis_index("row_1")
    own = row_pos()
    for block, out in ((own, keep_ref), (own + 1 - 2 * core, send_ref)):
        pieces = [s_ref[k, pl.ds(2 * block + e, 1), :] for k in range(2) for e in range(2)]
        pieces += [m_ref[h, pl.ds(block, 1), :] for h in range(4)]
        out[...] = jnp.concatenate(pieces, axis=0).astype(BF16)


def own_kernel(
    count_ref, v_ref, x_ref, xb_ref, w_ref, yb_ref, xs_ref, xv_ref, ys_ref, yc_ref,
    after_ref, own_ref, xc_ref, hc_ref, xx_ref, yy_ref, xo_ref, wm_ref,
):
    count = count_ref[0:1, 0:1]
    x_all = x_ref[...]
    n_in = 2 * (XW + 4)
    dst, src = iota((XW, n_in), 0), iota((XW, n_in), 1)
    row, col = iota((8, n_in), 0), iota((8, n_in), 1)
    row_x, row_y = iota((8, XW), 0), iota((8, YR), 0)
    row_h, col_h = iota((8, YR + 4), 0), iota((8, YR + 4), 1)
    slot_in, slot_out = iota((YR + 4, YR), 0), iota((YR + 4, YR), 1)
    shift = ones_where((slot_in == slot_out + 2) & (slot_out < count)).astype(BF16)

    def placed(values, offsets):
        found = jnp.where(values[0] == 4, offsets[0], -1)
        for h in range(1, 4):
            found = jnp.where(values[0] == 4 + h, offsets[h], found)
        return ones_where(values[1] == found).astype(BF16)

    x_high = xb_ref[...].astype(BF16).astype(F32)
    y_high = yb_ref[...].astype(BF16).astype(F32)
    pick_y = placed((row_h, col_h), (0, 1, YR + 2, YR + 3))
    for k in range(2):
        lanes = slice(XW * k, XW * k + XW)
        xo_ref[:, lanes] = nn(ones_where(src == 2 * (dst + 2) + k).astype(BF16), x_all).astype(BF16)
        pick_x = placed((row, col), [2 * h + k for h in HALO_X])
        mine = (row_x // 2) == k
        head = jnp.where(mine, x_high, F32(0.0)) + nn(pick_x, x_all)
        tail = jnp.where(mine, xb_ref[...] - x_high, F32(0.0))
        xc_ref[:, lanes] = jnp.concatenate([head, tail], axis=0).astype(BF16)
        wm_ref[k] = nn(w_ref[k], shift).astype(BF16)
        mine = (row_y // 2) == k
        head = jnp.where(mine, y_high, F32(0.0)) + nt(pick_y, w_ref[k])
        tail = jnp.where(mine, yb_ref[...] - y_high, F32(0.0))
        hc_ref[k] = jnp.concatenate([head, tail], axis=0).astype(BF16)
    yy_ref[...] = jnp.zeros_like(yy_ref)
    ys = ys_ref[...].reshape(1, YR)
    yy_ref[0:1, 0:YR] = ys
    yy_ref[1:2, 0:YR] = viscosity * yc_ref[...].reshape(1, YR)
    yy_ref[2:3, 0:YR] = viscosity * ys * ys
    scale, curv, y_second = (column_tiles(yy_ref, j) for j in range(3))
    xs, xv = xs_ref[...], viscosity * xv_ref[...]
    x_second = viscosity * xs * xs
    xx_ref[...] = jnp.concatenate([xs, xv, x_second, jnp.zeros((5, XW), F32)], axis=0)
    for pair in range(2):
        for f in range(3):
            plane = 4 * f + 2 * pair
            both = jnp.concatenate([v_ref[plane], v_ref[plane + 1]], axis=1)
            of_first, of_second = nn(wm_ref[0], both), nn(wm_ref[1], both)
            for j in range(2):
                p, z = plane + j, 2 * pair + j
                at = slice(XW * j, XW * j + XW)
                in_x = nn(v_ref[p], xo_ref[...])
                u, v = v_ref[z].astype(F32), v_ref[4 + z].astype(F32)
                rhs = (xv - u * xs) * in_x[:, 0:XW] + x_second * in_x[:, XW:]
                rhs = rhs + (curv - v * scale) * of_first[:, at]
                own_ref[p] = rhs + y_second * of_second[:, at]


def y_add_kernel(other, coef_ref, v_ref, own_ref, hc_ref, yy_ref, o_ref):
    core = lax.axis_index("row_1")
    half = 1 - core if other else core
    scale, curv, y_second = (column_tiles(yy_ref, j) for j in range(3))
    for g in range(0, HALF, 2):
        coef = coef_ref[:, 128 * g : 128 * g + 256].astype(F32)
        coef = jnp.concatenate([coef, coef], axis=0).astype(BF16)
        of_first, of_second = tn(hc_ref[0], coef), tn(hc_ref[1], coef)
        for j in range(2):
            p = HALF * half + g + j
            at = slice(128 * j, 128 * j + 128)
            v = v_ref[4 + lax.rem(p, 4)].astype(F32)
            add = (curv - v * scale) * of_first[:, at] + y_second * of_second[:, at]
            o_ref[p] = own_ref[p] + add


def finish_kernel(
    count_ref, c_ref, v_ref, p_ref, base_ref, xc_ref, xx_ref, rhs_hbm, inc_hbm,
    x_add, t_ref, rhs_ref, inc_ref, sems,
):
    count = count_ref[0:1, 0:1]
    t_ref[...] = c_ref[...].astype(F32).reshape(8 * NCOL, 128)
    top = top_of(t_ref, 0, NCOL, 8)
    spare = iota((1, 128), 1) >= CHUNK
    top = jnp.max(jnp.where(spare, top, F32(0.0)), axis=1, keepdims=True)
    step = cfl_target / (top + 1e-06)
    gamma_step, zeta_step = gamma_coef * step, zeta_coef * step
    x_corr = xc_ref[...]
    live = iota((YR, XW), 0) < count
    xs, xv, x_second = xx_ref[0:1, :], xx_ref[1:2, :], xx_ref[2:3, :]
    done, copies = 0, []
    for p in range(NP):
        while done < CHUNKS and CHUNK * done < YR * (p + 1):
            coef = t_ref[8 * done : 8 * done + 8, :]
            coef = jnp.concatenate([coef, coef], axis=0).astype(BF16)
            x_add[CHUNK * done : CHUNK * done + 128, :] = tn(coef, x_corr)
            done += 1
        u = v_ref[p % 4].astype(F32)
        add = x_add[YR * p : YR * p + YR, :]
        rhs = (xv - u * xs) * add[:, 0:XW] + x_second * add[:, XW:]
        rhs = jnp.where(live, base_ref[p] + rhs, F32(0.0))
        before = jnp.where(live, zeta_step, F32(0.0)) * p_ref[p].astype(F32)
        rhs_ref[p] = rhs.astype(BF16)
        inc_ref[p] = (gamma_step * rhs + before).astype(BF16)
        if (p + 1) % GROUP == 0:
            group = pl.ds(p + 1 - GROUP, GROUP)
            for j, (source, target) in enumerate(((rhs_ref, rhs_hbm), (inc_ref, inc_hbm))):
                sem = sems.at[j, p // GROUP]
                copies.append(pltpu.make_async_copy(source.at[group], target.at[group], sem))
                copies[-1].start()
    for copy in copies:
        copy.wait()


VMEM = pl.BlockSpec(memory_space=pltpu.VMEM)
HBM = pl.BlockSpec(memory_space=pltpu.HBM)


def call(body, name, operands, outs, scratch=(), flops=0, mib=6, far=(), far_outs=(), alias=None):
    specs = [HBM if j in far else VMEM for j in range(len(operands))]
    size = sum(o.size * o.dtype.itemsize for o in operands)
    single = len(outs) == 1
    out_specs = [HBM if j in far_outs else VMEM for j in range(len(outs))]
    return pl.pallas_call(
        body,
        out_shape=outs[0] if single else outs,
        in_specs=specs,
        out_specs=out_specs[0] if single else out_specs,
        scratch_shapes=[pltpu.VMEM(item, F32) if isinstance(item, tuple) else item for item in scratch],
        compiler_params=pltpu.CompilerParams(vmem_limit_bytes=mib * 2**20),
        cost_estimate=pl.CostEstimate(flops=flops, bytes_accessed=size, transcendentals=0),
        input_output_aliases=alias or {},
        name=name,
    )(*operands)


def shape(dims, kind=BF16):
    return jax.ShapeDtypeStruct(dims, kind)


def shards(
    velocity, rhs_prev, row_counts, x_scale, x_curv, y_scale, y_curv,
    x_local, x_coupling, x_basis, y_local, y_coupling, y_basis,
):
    lines = velocity.reshape(LINES, XW)
    previous = rhs_prev.reshape(NP, YR, XW)
    x_rows = x_local.reshape(2 * (XW + 4), XW)
    y_mats = jnp.transpose(y_local, (1, 2, 0))
    x_scale, x_curv = x_scale.reshape(1, XW), x_curv.reshape(1, XW)

    fetched = (lines, x_rows, y_mats, x_scale, y_scale)
    *fetched, row_counts = [
        pltpu.with_memory_space_constraint(item, pltpu.HBM) for item in (*fetched, row_counts)
    ]
    mine, lines, x_rows, y_mats, x_scale, y_scale, count = call(
        x_partial_kernel, "x_partial", (*fetched, row_counts),
        (
            shape((NCOL, 8, 128)), *(pltpu.VMEM(item.shape, item.dtype) for item in fetched),
            pltpu.VMEM((8, 128), jnp.int32),
        ),
        (pltpu.SMEM((NROW,), jnp.int32), pltpu.SemaphoreType.DMA((6,))),
        flops=10**8, far=range(6),
    )
    planes = lines.reshape(NP, YR, XW)
    theirs = lax.all_to_all(mine, COL, 0, 0, tiled=True)
    y_part = call(
        y_partial_kernel, "y_partial", (count, planes, y_mats, x_scale, y_scale),
        (shape((NROW, 8 * TILES, 128)),), ((16, 384),), flops=10**8,
    )
    x_basis = jnp.pad(x_basis.reshape(4, XW), ((0, 4), (0, 0)))
    y_basis = jnp.pad(y_basis.reshape(4, YR), ((0, 4), (0, 0)))
    columns = lax.all_to_all(y_part, ROW, 0, 0, tiled=True)
    x_solved = call(
        x_solve_kernel, "x_solve", (theirs, x_rows, x_coupling), (shape((NCOL, 8, 128)),),
        ((NCOL * 8, 128), (2, 2 * NCOL, 128), (2, 2 * NCOL, 128)), flops=10**8,
    )
    own, x_corr, y_corr, x_lines, y_lines = call(
        own_kernel, "own",
        (count, planes, x_rows, x_basis, y_mats, y_basis, x_scale, x_curv, y_scale, y_curv,
            y_part),
        (
            shape((NP, YR, XW), F32), shape((16, 2 * XW)), shape((2, 16, YR)),
            shape((8, XW), F32), shape((8, 384), F32),
        ),
        (pltpu.VMEM((XW, 2 * XW), BF16), pltpu.VMEM((2, YR, YR), BF16)),
        flops=6 * 10**8, mib=8, far=(10,),
    )
    x_back = call(
        top_kernel, "top", (x_solved, columns, x_lines), (shape((NCOL, 8, 128)),),
        ((8 * NROW, 128),), far=(2,),
    )
    x_back = lax.all_to_all(x_back, COL, 0, 0, tiled=True)
    wide = 128 * HALF
    keep, send = call(
        y_solve_kernel, "y_solve", (columns, y_coupling), (shape((8, wide)), shape((8, wide))),
        (
            (NROW * 8 * TILES, 128), (NP, 2 * NROW, 128), (2, 2 * NROW, wide), (4, NROW, wide),
        ), flops=10**8,
    )
    got = lax.ppermute(send, "row_1", [(0, 1), (1, 0)])
    base = own
    for other, coefs in enumerate((keep, got)):
        base = call(
            functools.partial(y_add_kernel, other), "y_add",
            (coefs, planes, base, y_corr, y_lines),
            (shape(own.shape, F32),), flops=10**8, alias={2: 0},
        )
    rhs, inc = call(
        finish_kernel, "finish",
        (count, x_back, planes, previous, base, x_corr, x_lines),
        (shape((NP, YR, XW)), shape((NP, YR, XW))),
        (
            (CHUNK * (CHUNKS - 1) + 128, 2 * XW), (8 * NCOL, 128),
            pltpu.VMEM((NP, YR, XW), BF16), pltpu.VMEM((NP, YR, XW), BF16),
            pltpu.SemaphoreType.DMA((2, NP // GROUP)),
        ), flops=10**8, mib=10, far_outs=(0, 1),
    )
    return rhs.reshape(velocity.shape), inc.reshape(velocity.shape)


def solution(mesh):
    torus = Mesh(mesh.devices.reshape(8, 2, 8, 4), ("row_0", "row_1", "col_0", "col_1"))
    placed = (
        P(None, None, ROW, COL), P(None, None, ROW, COL), P(), P(COL), P(COL), P(ROW), P(ROW),
        P(), P(), P(), P(ROW, None, None), P(), P(ROW, None, None, None),
    )
    return jax.shard_map(
        shards,
        mesh=torus,
        in_specs=placed,
        out_specs=(P(None, None, ROW, COL), P(None, None, ROW, COL)),
        check_vma=False,
    )
```

```python
import jax
import jax.numpy as jnp
from jax import lax
from jax.experimental import pallas as pl
from jax.experimental.pallas import tpu as pltpu
from jax.sharding import Mesh
from jax.sharding import PartitionSpec as P

COL = ("col_0", "col_1")
ROW = ("row_0", "row_1")

viscosity = 0.1
cfl_target = 1.5
gamma_coef = 5.0 / 12.0
zeta_coef = -17.0 / 60.0

F32 = jnp.float32
BF16 = jnp.bfloat16
NCOL = 32
NROW = 16
XW = 128
YR = 264
NP = 12
LINES = NP * YR
CHUNK = 112
CHUNKS = -(-LINES // CHUNK)
TILES = NP + 1
GROUP = 4
EDGE_X = (0, 1, XW - 2, XW - 1)
HALO_X = (0, 1, XW + 2, XW + 3)


def nn(a, b, precision=None):
    return lax.dot_general(
        a, b, (((1,), (0,)), ((), ())), precision=precision, preferred_element_type=F32
    )


def nt(a, b):
    return lax.dot_general(a, b, (((1,), (1,)), ((), ())), preferred_element_type=F32)


def tn(a, b):
    return lax.dot_general(a, b, (((0,), (0,)), ((), ())), preferred_element_type=F32)


def iota(shape, dim):
    return lax.broadcasted_iota(jnp.int32, shape, dim)


def ones_where(cond):
    return jnp.where(cond, F32(1.0), F32(0.0))


def row_pos():
    return lax.axis_index("row_0") * 2 + lax.axis_index("row_1")


def three_parts(value):
    high = value.astype(BF16).astype(F32)
    rest = value - high
    mid = rest.astype(BF16).astype(F32)
    return high, mid, rest - mid


def max_tile(value):
    high, mid, low = three_parts(jnp.broadcast_to(value, (8, 128)))
    row = iota((8, 128), 0)
    return jnp.where(
        row == 0, high, jnp.where(row == 1, mid, jnp.where(row == 2, low, F32(0.0)))
    )


def column_tiles(row_ref, row):
    pieces = []
    for j in range(3):
        seg = row_ref[row : row + 1, 128 * j : 128 * j + 128]
        pieces.append(jnp.transpose(jnp.broadcast_to(seg, (128, 128))))
    return jnp.concatenate([pieces[0], pieces[1], pieces[2][0 : YR - 256]], axis=0)


def x_partial_kernel(
    v_hbm, x_hbm, w_hbm, xs_hbm, ys_hbm, count_hbm,
    o_ref, v_ref, x_ref, w_ref, xs_ref, ys_ref, count_ref, counts, sems,
):
    copies = [
        pltpu.make_async_copy(x_hbm, x_ref, sems.at[0]), pltpu.make_async_copy(v_hbm, v_ref, sems.at[1])
    ]
    later = ((w_hbm, w_ref), (xs_hbm, xs_ref), (ys_hbm, ys_ref), (count_hbm, counts))
    later = [pltpu.make_async_copy(*pair, sems.at[2 + j]) for j, pair in enumerate(later)]
    for copy in copies + later:
        copy.start()
    row, lane = iota((8, XW), 0), iota((8, XW), 1)
    pick = ones_where((row < 4) & (lane == (XW - 1) * (row % 2))).astype(BF16)
    row_e = iota((8, 2 * (XW + 4)), 0)
    edges = jnp.where(row == 4, ones_where(lane == EDGE_X[0]), F32(0.0))
    for j in range(1, 4):
        edges = jnp.where(row == 4 + j, ones_where(lane == EDGE_X[j]), edges)
    src, dst = iota((2 * (XW + 4), XW), 0), iota((2 * (XW + 4), XW), 1)
    spread = ones_where(src // 2 == dst + 2).astype(BF16)
    mine = iota((8, 2 * (XW + 4)), 1) % 2 == row_e // 2
    copies[0].wait()
    ends = jnp.where(mine, nt(pick, x_ref[...]), F32(0.0)).astype(BF16)
    weights = (edges + nn(ends, spread)).astype(BF16)
    o_ref[CHUNKS:] = jnp.zeros((NCOL - CHUNKS, 8, 128), BF16)
    copies[1].wait()
    for d in range(0, NCOL, 2):
        first = CHUNK * d
        last = min(first + 256, LINES)
        if last - first == 256:
            pair = nt(weights, v_ref[first:last, :])
            o_ref[d] = pair[:, 0:128].astype(BF16)
            o_ref[d + 1] = pltpu.roll(pair, 256 - CHUNK, 1)[:, 0:128].astype(BF16)
        elif last > first:
            part = nt(weights, v_ref[first:last, :])
            rest = jnp.zeros((8, 128 - (last - first)), F32)
            o_ref[d] = jnp.concatenate([part, rest], axis=1).astype(BF16)
    for copy in later:
        copy.wait()
    count_ref[...] = jnp.full((8, 128), counts[row_pos()], jnp.int32)


def y_partial_kernel(count_ref, v_ref, w_ref, xs_ref, ys_ref, o_ref, pad_ref):
    count = count_ref[0:1, 0:1]
    row, slot = iota((8, YR), 0), iota((8, YR), 1)
    place = jnp.where(row % 2 == 0, 0, count - 1)
    ends = nn(ones_where((row < 2) & (slot == place)).astype(BF16), w_ref[0])
    ends = ends + nn(
        ones_where((row >= 2) & (row < 4) & (slot == place)).astype(BF16), w_ref[1]
    )
    pad_ref[...] = jnp.zeros_like(pad_ref)
    pad_ref[0:8, 0 : YR + 4] = ends
    pad_ref[8:9, 0:YR] = ys_ref[...].reshape(1, YR)
    wide = pad_ref[0:8, :]
    own = pltpu.roll(wide, 384 - 2, 1)[:, 0:YR]
    edge = jnp.where(
        row == 4, 0, jnp.where(row == 5, 1, jnp.where(row == 6, count - 2, count - 1))
    )
    weights = jnp.where(
        row < 4, jnp.where(slot < count, own, F32(0.0)), ones_where(slot == edge)
    ).astype(BF16)
    lane8, row8 = iota((8, 128), 1), iota((8, 128), 0)
    margin = jnp.where(
        lane8 < 2, wide[:, 0:128], pltpu.roll(wide[:, 256:384], 128 - (YR - 256), 1)
    )
    ys = column_tiles(pad_ref, 8)
    live = iota((YR, XW), 0) < count
    top = jnp.zeros((YR, XW), F32)
    for z in range(4):
        speed = jnp.abs(v_ref[z].astype(F32)) * xs_ref[...]
        speed = speed + jnp.abs(v_ref[4 + z].astype(F32)) * ys
        top = jnp.maximum(top, speed)
    top = jnp.where(live, top, F32(0.0))
    top = jnp.max(jnp.max(top, axis=0, keepdims=True), axis=1, keepdims=True)
    last = jnp.where(row8 < 4, margin, pltpu.roll(max_tile(top), 4, 0))
    tiles = [nn(weights, v_ref[p]) for p in range(NP)]
    o_ref[0] = jnp.concatenate(tiles + [last], axis=0).astype(BF16)


def top_of(ref, first, count, stride):
    parts = [ref[pl.ds(first + j, count, stride=stride), :] for j in range(3)]
    return jnp.max(parts[0] + parts[1] + parts[2], axis=0, keepdims=True)


def x_solve_kernel(c_ref, x_ref, coupling_ref, r_ref, o_ref, a_ref, e_ref, s_ref, t_ref):
    a_ref[...] = c_ref[...].astype(F32).reshape(NCOL * 8, 128)
    part = [a_ref[pl.ds(v, NCOL, stride=8), :] for v in range(8)]
    margin = [pltpu.roll(part[6], 1, 0), pltpu.roll(part[7], 1, 0)]
    margin += [pltpu.roll(part[4], NCOL - 1, 0), pltpu.roll(part[5], NCOL - 1, 0)]
    local = x_ref[...].astype(F32)
    for k in range(2):
        for e in range(2):
            ends = part[2 * k + e]
            lane = (XW - 1) * e
            for h in range(4):
                place = 2 * HALO_X[h] + k
                ends = ends + local[place : place + 1, lane : lane + 1] * margin[h]
            e_ref[k, pl.ds(e, NCOL, stride=2), :] = ends
        s_ref[k] = nn(coupling_ref[k], e_ref[k], lax.Precision.HIGHEST)
        for e in range(2):
            a_ref[pl.ds(2 * k + e, NCOL, stride=8), :] = s_ref[k, pl.ds(e, NCOL, stride=2), :]
    for h in range(4):
        a_ref[pl.ds(4 + h, NCOL, stride=8), :] = margin[h]
    t_ref[...] = r_ref[...][:, 8 * NP : 8 * TILES, :].astype(F32).reshape(8 * NROW, 128)
    tile = max_tile(top_of(t_ref, 4, NROW, 8))
    spare = iota((8, 128), 1) >= CHUNK
    solved = a_ref[...].reshape(NCOL, 8, 128)
    o_ref[...] = jnp.where(spare[None], tile[None], solved).astype(BF16)


def y_solve_kernel(r_ref, coupling_ref, o_ref, a_ref, e_ref, s_ref, m_ref):
    a_ref[...] = r_ref[...].astype(F32).reshape(NROW * 8 * TILES, 128)

    def rows_of(place):
        return a_ref[pl.ds(place, NROW, stride=8 * TILES), :]

    source = iota((NROW, 128), 0)
    weights = [rows_of(8 * NP + j) for j in range(4)]
    weight = [
        [jnp.broadcast_to(weights[j][:, h : h + 1], (NROW, 128)) for h in range(4)]
        for j in range(4)
    ]
    for g in range(NP):
        lanes = slice(128 * g, 128 * g + 128)
        part = [rows_of(8 * g + v) for v in range(8)]
        margin = [pltpu.roll(part[6 + h], 1, 0) for h in range(2)]
        margin = [jnp.where(source == 0, F32(0.0), m) for m in margin]
        upper = [pltpu.roll(part[4 + h], NROW - 1, 0) for h in range(2)]
        margin += [jnp.where(source == NROW - 1, F32(0.0), m) for m in upper]
        for h in range(4):
            m_ref[h, :, lanes] = margin[h]
        for k in range(2):
            for e in range(2):
                ends = part[2 * k + e]
                for h in range(4):
                    ends = ends + weight[2 * k + e][h] * margin[h]
                e_ref[NP * k + g, pl.ds(e, NROW, stride=2), :] = ends
    for k in range(2):
        ends = jnp.concatenate([e_ref[NP * k + g] for g in range(NP)], axis=1)
        s_ref[k] = nn(coupling_ref[k], ends, lax.Precision.HIGHEST)
    own = row_pos()
    pieces = [s_ref[k, pl.ds(2 * own + e, 1), :] for k in range(2) for e in range(2)]
    pieces += [m_ref[h, pl.ds(own, 1), :] for h in range(4)]
    o_ref[...] = jnp.concatenate(pieces, axis=0).astype(BF16)


def own_kernel(
    count_ref, v_ref, x_ref, xb_ref, w_ref, yb_ref, xs_ref, xv_ref, ys_ref, yc_ref,
    after_ref, own_ref, xc_ref, hc_ref, xx_ref, yy_ref, xo_ref, wm_ref,
):
    count = count_ref[0:1, 0:1]
    x_all = x_ref[...]
    n_in = 2 * (XW + 4)
    dst, src = iota((XW, n_in), 0), iota((XW, n_in), 1)
    row, col = iota((8, n_in), 0), iota((8, n_in), 1)
    row_x, row_y = iota((8, XW), 0), iota((8, YR), 0)
    row_h, col_h = iota((8, YR + 4), 0), iota((8, YR + 4), 1)
    slot_in, slot_out = iota((YR + 4, YR), 0), iota((YR + 4, YR), 1)
    shift = ones_where((slot_in == slot_out + 2) & (slot_out < count)).astype(BF16)

    def placed(values, offsets):
        found = jnp.where(values[0] == 4, offsets[0], -1)
        for h in range(1, 4):
            found = jnp.where(values[0] == 4 + h, offsets[h], found)
        return ones_where(values[1] == found).astype(BF16)

    x_high = xb_ref[...].astype(BF16).astype(F32)
    y_high = yb_ref[...].astype(BF16).astype(F32)
    pick_y = placed((row_h, col_h), (0, 1, YR + 2, YR + 3))
    for k in range(2):
        lanes = slice(XW * k, XW * k + XW)
        xo_ref[:, lanes] = nn(ones_where(src == 2 * (dst + 2) + k).astype(BF16), x_all).astype(BF16)
        pick_x = placed((row, col), [2 * h + k for h in HALO_X])
        mine = (row_x // 2) == k
        head = jnp.where(mine, x_high, F32(0.0)) + nn(pick_x, x_all)
        tail = jnp.where(mine, xb_ref[...] - x_high, F32(0.0))
        xc_ref[:, lanes] = jnp.concatenate([head, tail], axis=0).astype(BF16)
        wm_ref[k] = nn(w_ref[k], shift).astype(BF16)
        mine = (row_y // 2) == k
        head = jnp.where(mine, y_high, F32(0.0)) + nt(pick_y, w_ref[k])
        tail = jnp.where(mine, yb_ref[...] - y_high, F32(0.0))
        hc_ref[k] = jnp.concatenate([head, tail], axis=0).astype(BF16)
    yy_ref[...] = jnp.zeros_like(yy_ref)
    ys = ys_ref[...].reshape(1, YR)
    yy_ref[0:1, 0:YR] = ys
    yy_ref[1:2, 0:YR] = viscosity * yc_ref[...].reshape(1, YR)
    yy_ref[2:3, 0:YR] = viscosity * ys * ys
    scale, curv, y_second = (column_tiles(yy_ref, j) for j in range(3))
    xs, xv = xs_ref[...], viscosity * xv_ref[...]
    x_second = viscosity * xs * xs
    xx_ref[...] = jnp.concatenate([xs, xv, x_second, jnp.zeros((5, XW), F32)], axis=0)
    for pair in range(2):
        for f in range(3):
            plane = 4 * f + 2 * pair
            both = jnp.concatenate([v_ref[plane], v_ref[plane + 1]], axis=1)
            of_first, of_second = nn(wm_ref[0], both), nn(wm_ref[1], both)
            for j in range(2):
                p, z = plane + j, 2 * pair + j
                at = slice(XW * j, XW * j + XW)
                in_x = nn(v_ref[p], xo_ref[...])
                u, v = v_ref[z].astype(F32), v_ref[4 + z].astype(F32)
                rhs = (xv - u * xs) * in_x[:, 0:XW] + x_second * in_x[:, XW:]
                rhs = rhs + (curv - v * scale) * of_first[:, at]
                own_ref[p] = rhs + y_second * of_second[:, at]


def y_add_kernel(coef_ref, v_ref, own_ref, hc_ref, yy_ref, o_ref):
    scale, curv, y_second = (column_tiles(yy_ref, j) for j in range(3))
    for pair in range(0, NP, 2):
        coef = coef_ref[:, 128 * pair : 128 * pair + 256].astype(F32)
        coef = jnp.concatenate([coef, coef], axis=0).astype(BF16)
        of_first, of_second = tn(hc_ref[0], coef), tn(hc_ref[1], coef)
        for j in range(2):
            p = pair + j
            at = slice(128 * j, 128 * j + 128)
            v = v_ref[4 + p % 4].astype(F32)
            add = (curv - v * scale) * of_first[:, at] + y_second * of_second[:, at]
            o_ref[p] = own_ref[p] + add


def finish_kernel(
    count_ref, c_ref, v_ref, p_ref, base_ref, xc_ref, xx_ref, rhs_hbm, inc_hbm,
    x_add, t_ref, rhs_ref, inc_ref, sems,
):
    count = count_ref[0:1, 0:1]
    t_ref[...] = c_ref[...].astype(F32).reshape(8 * NCOL, 128)
    top = top_of(t_ref, 0, NCOL, 8)
    spare = iota((1, 128), 1) >= CHUNK
    top = jnp.max(jnp.where(spare, top, F32(0.0)), axis=1, keepdims=True)
    step = cfl_target / (top + 1e-06)
    gamma_step, zeta_step = gamma_coef * step, zeta_coef * step
    x_corr = xc_ref[...]
    live = iota((YR, XW), 0) < count
    xs, xv, x_second = xx_ref[0:1, :], xx_ref[1:2, :], xx_ref[2:3, :]
    done, copies = 0, []
    for p in range(NP):
        while done < CHUNKS and CHUNK * done < YR * (p + 1):
            coef = t_ref[8 * done : 8 * done + 8, :]
            coef = jnp.concatenate([coef, coef], axis=0).astype(BF16)
            x_add[CHUNK * done : CHUNK * done + 128, :] = tn(coef, x_corr)
            done += 1
        u = v_ref[p % 4].astype(F32)
        add = x_add[YR * p : YR * p + YR, :]
        rhs = (xv - u * xs) * add[:, 0:XW] + x_second * add[:, XW:]
        rhs = jnp.where(live, base_ref[p] + rhs, F32(0.0))
        before = jnp.where(live, zeta_step, F32(0.0)) * p_ref[p].astype(F32)
        rhs_ref[p] = rhs.astype(BF16)
        inc_ref[p] = (gamma_step * rhs + before).astype(BF16)
        if (p + 1) % GROUP == 0:
            group = pl.ds(p + 1 - GROUP, GROUP)
            for j, (source, target) in enumerate(((rhs_ref, rhs_hbm), (inc_ref, inc_hbm))):
                sem = sems.at[j, p // GROUP]
                copies.append(pltpu.make_async_copy(source.at[group], target.at[group], sem))
                copies[-1].start()
    for copy in copies:
        copy.wait()


VMEM = pl.BlockSpec(memory_space=pltpu.VMEM)
HBM = pl.BlockSpec(memory_space=pltpu.HBM)


def call(body, name, operands, outs, scratch=(), flops=0, mib=6, far=(), far_outs=(), alias=None):
    specs = [HBM if j in far else VMEM for j in range(len(operands))]
    size = sum(o.size * o.dtype.itemsize for o in operands)
    single = len(outs) == 1
    out_specs = [HBM if j in far_outs else VMEM for j in range(len(outs))]
    return pl.pallas_call(
        body,
        out_shape=outs[0] if single else outs,
        in_specs=specs,
        out_specs=out_specs[0] if single else out_specs,
        scratch_shapes=[pltpu.VMEM(item, F32) if isinstance(item, tuple) else item for item in scratch],
        compiler_params=pltpu.CompilerParams(vmem_limit_bytes=mib * 2**20),
        cost_estimate=pl.CostEstimate(flops=flops, bytes_accessed=size, transcendentals=0),
        input_output_aliases=alias or {},
        name=name,
    )(*operands)


def shape(dims, kind=BF16):
    return jax.ShapeDtypeStruct(dims, kind)


def shards(
    velocity, rhs_prev, row_counts, x_scale, x_curv, y_scale, y_curv,
    x_local, x_coupling, x_basis, y_local, y_coupling, y_basis,
):
    lines = velocity.reshape(LINES, XW)
    previous = rhs_prev.reshape(NP, YR, XW)
    x_rows = x_local.reshape(2 * (XW + 4), XW)
    y_mats = jnp.transpose(y_local, (1, 2, 0))
    x_scale, x_curv = x_scale.reshape(1, XW), x_curv.reshape(1, XW)

    fetched = (lines, x_rows, y_mats, x_scale, y_scale)
    *fetched, row_counts = [
        pltpu.with_memory_space_constraint(item, pltpu.HBM) for item in (*fetched, row_counts)
    ]
    mine, lines, x_rows, y_mats, x_scale, y_scale, count = call(
        x_partial_kernel, "x_partial", (*fetched, row_counts),
        (
            shape((NCOL, 8, 128)), *(pltpu.VMEM(item.shape, item.dtype) for item in fetched),
            pltpu.VMEM((8, 128), jnp.int32),
        ),
        (pltpu.SMEM((NROW,), jnp.int32), pltpu.SemaphoreType.DMA((6,))),
        flops=10**8, far=range(6),
    )
    planes = lines.reshape(NP, YR, XW)
    theirs = lax.all_to_all(mine, COL, 0, 0, tiled=True)
    y_part = call(
        y_partial_kernel, "y_partial", (count, planes, y_mats, x_scale, y_scale),
        (shape((1, 8 * TILES, 128)),), ((16, 384),), flops=10**8,
    )
    columns = lax.all_gather(y_part, ROW, axis=0, tiled=True)
    x_basis = jnp.pad(x_basis.reshape(4, XW), ((0, 4), (0, 0)))
    y_basis = jnp.pad(y_basis.reshape(4, YR), ((0, 4), (0, 0)))
    x_solved = call(
        x_solve_kernel, "x_solve", (theirs, x_rows, x_coupling, columns), (shape((NCOL, 8, 128)),),
        ((NCOL * 8, 128), (2, 2 * NCOL, 128), (2, 2 * NCOL, 128), (8 * NROW, 128)), flops=10**8,
    )
    x_back = lax.all_to_all(x_solved, COL, 0, 0, tiled=True)
    own, x_corr, y_corr, x_lines, y_lines = call(
        own_kernel, "own",
        (
            count, planes, x_rows, x_basis, y_mats, y_basis, x_scale, x_curv, y_scale, y_curv,
            x_solved,
        ),
        (
            shape((NP, YR, XW), F32), shape((16, 2 * XW)), shape((2, 16, YR)),
            shape((8, XW), F32), shape((8, 384), F32),
        ),
        (pltpu.VMEM((XW, 2 * XW), BF16), pltpu.VMEM((2, YR, YR), BF16)),
        flops=6 * 10**8, mib=8, far=(10,),
    )
    wide = 128 * NP
    y_solved = call(
        y_solve_kernel, "y_solve", (columns, y_coupling), (shape((8, wide)),),
        (
            (NROW * 8 * TILES, 128), (2 * NP, 2 * NROW, 128), (2, 2 * NROW, wide), (4, NROW, wide),
        ), flops=10**8,
    )
    base = call(
        y_add_kernel, "y_add", (y_solved, planes, own, y_corr, y_lines),
        (shape(own.shape, F32),), flops=10**8, alias={2: 0},
    )
    rhs, inc = call(
        finish_kernel, "finish",
        (count, x_back, planes, previous, base, x_corr, x_lines),
        (shape((NP, YR, XW)), shape((NP, YR, XW))),
        (
            (CHUNK * (CHUNKS - 1) + 128, 2 * XW), (8 * NCOL, 128),
            pltpu.VMEM((NP, YR, XW), BF16), pltpu.VMEM((NP, YR, XW), BF16),
            pltpu.SemaphoreType.DMA((2, NP // GROUP)),
        ), flops=10**8, mib=10, far_outs=(0, 1),
    )
    return rhs.reshape(velocity.shape), inc.reshape(velocity.shape)


def solution(mesh):
    torus = Mesh(mesh.devices.reshape(8, 2, 8, 4), ("row_0", "row_1", "col_0", "col_1"))
    placed = (
        P(None, None, ROW, COL), P(None, None, ROW, COL), P(), P(COL), P(COL), P(ROW), P(ROW),
        P(), P(), P(), P(ROW, None, None), P(), P(ROW, None, None, None),
    )
    return jax.shard_map(
        shards,
        mesh=torus,
        in_specs=placed,
        out_specs=(P(None, None, ROW, COL), P(None, None, ROW, COL)),
        check_vma=False,
    )
```

```python
import jax
import jax.numpy as jnp
from jax import lax
from jax.experimental import pallas as pl
from jax.experimental.pallas import tpu as pltpu
from jax.sharding import Mesh
from jax.sharding import PartitionSpec as P

COL = ("col_0", "col_1")
ROW = ("row_0", "row_1")

viscosity = 0.1
cfl_target = 1.5
gamma_coef = 5.0 / 12.0
zeta_coef = -17.0 / 60.0

F32 = jnp.float32
BF16 = jnp.bfloat16
NCOL = 32
NROW = 16
XW = 128
YR = 264
NP = 12
LINES = NP * YR
CHUNK = 112
CHUNKS = -(-LINES // CHUNK)
TILES = NP + 1
GROUP = 4
EDGE_X = (0, 1, XW - 2, XW - 1)
HALO_X = (0, 1, XW + 2, XW + 3)


def nn(a, b, precision=None):
    return lax.dot_general(
        a, b, (((1,), (0,)), ((), ())), precision=precision, preferred_element_type=F32
    )


def nt(a, b):
    return lax.dot_general(a, b, (((1,), (1,)), ((), ())), preferred_element_type=F32)


def tn(a, b):
    return lax.dot_general(a, b, (((0,), (0,)), ((), ())), preferred_element_type=F32)


def iota(shape, dim):
    return lax.broadcasted_iota(jnp.int32, shape, dim)


def ones_where(cond):
    return jnp.where(cond, F32(1.0), F32(0.0))


def row_pos():
    return lax.axis_index("row_0") * 2 + lax.axis_index("row_1")


def three_parts(value):
    high = value.astype(BF16).astype(F32)
    rest = value - high
    mid = rest.astype(BF16).astype(F32)
    return high, mid, rest - mid


def max_tile(value):
    high, mid, low = three_parts(jnp.broadcast_to(value, (8, 128)))
    row = iota((8, 128), 0)
    return jnp.where(
        row == 0, high, jnp.where(row == 1, mid, jnp.where(row == 2, low, F32(0.0)))
    )


def column_tiles(row_ref, row):
    pieces = []
    for j in range(3):
        seg = row_ref[row : row + 1, 128 * j : 128 * j + 128]
        pieces.append(jnp.transpose(jnp.broadcast_to(seg, (128, 128))))
    return jnp.concatenate([pieces[0], pieces[1], pieces[2][0 : YR - 256]], axis=0)


def x_partial_kernel(
    v_hbm, x_hbm, w_hbm, xs_hbm, ys_hbm, count_hbm,
    o_ref, v_ref, x_ref, w_ref, xs_ref, ys_ref, count_ref, counts, sems,
):
    copies = [
        pltpu.make_async_copy(x_hbm, x_ref, sems.at[0]), pltpu.make_async_copy(v_hbm, v_ref, sems.at[1])
    ]
    later = ((w_hbm, w_ref), (xs_hbm, xs_ref), (ys_hbm, ys_ref), (count_hbm, counts))
    later = [pltpu.make_async_copy(*pair, sems.at[2 + j]) for j, pair in enumerate(later)]
    for copy in copies + later:
        copy.start()
    row, lane = iota((8, XW), 0), iota((8, XW), 1)
    pick = ones_where((row < 4) & (lane == (XW - 1) * (row % 2))).astype(BF16)
    row_e = iota((8, 2 * (XW + 4)), 0)
    edges = jnp.where(row == 4, ones_where(lane == EDGE_X[0]), F32(0.0))
    for j in range(1, 4):
        edges = jnp.where(row == 4 + j, ones_where(lane == EDGE_X[j]), edges)
    src, dst = iota((2 * (XW + 4), XW), 0), iota((2 * (XW + 4), XW), 1)
    spread = ones_where(src // 2 == dst + 2).astype(BF16)
    mine = iota((8, 2 * (XW + 4)), 1) % 2 == row_e // 2
    copies[0].wait()
    ends = jnp.where(mine, nt(pick, x_ref[...]), F32(0.0)).astype(BF16)
    weights = (edges + nn(ends, spread)).astype(BF16)
    o_ref[CHUNKS:] = jnp.zeros((NCOL - CHUNKS, 8, 128), BF16)
    copies[1].wait()
    for d in range(0, NCOL, 2):
        first = CHUNK * d
        last = min(first + 256, LINES)
        if last - first == 256:
            pair = nt(weights, v_ref[first:last, :])
            o_ref[d] = pair[:, 0:128].astype(BF16)
            o_ref[d + 1] = pltpu.roll(pair, 256 - CHUNK, 1)[:, 0:128].astype(BF16)
        elif last > first:
            part = nt(weights, v_ref[first:last, :])
            rest = jnp.zeros((8, 128 - (last - first)), F32)
            o_ref[d] = jnp.concatenate([part, rest], axis=1).astype(BF16)
    for copy in later:
        copy.wait()
    count_ref[...] = jnp.full((8, 128), counts[row_pos()], jnp.int32)


def y_partial_kernel(count_ref, v_ref, w_ref, xs_ref, ys_ref, o_ref, pad_ref):
    count = count_ref[0:1, 0:1]
    row, slot = iota((8, YR), 0), iota((8, YR), 1)
    place = jnp.where(row % 2 == 0, 0, count - 1)
    ends = nn(ones_where((row < 2) & (slot == place)).astype(BF16), w_ref[0])
    ends = ends + nn(
        ones_where((row >= 2) & (row < 4) & (slot == place)).astype(BF16), w_ref[1]
    )
    pad_ref[...] = jnp.zeros_like(pad_ref)
    pad_ref[0:8, 0 : YR + 4] = ends
    pad_ref[8:9, 0:YR] = ys_ref[...].reshape(1, YR)
    wide = pad_ref[0:8, :]
    own = pltpu.roll(wide, 384 - 2, 1)[:, 0:YR]
    edge = jnp.where(
        row == 4, 0, jnp.where(row == 5, 1, jnp.where(row == 6, count - 2, count - 1))
    )
    weights = jnp.where(
        row < 4, jnp.where(slot < count, own, F32(0.0)), ones_where(slot == edge)
    ).astype(BF16)
    lane8, row8 = iota((8, 128), 1), iota((8, 128), 0)
    margin = jnp.where(
        lane8 < 2, wide[:, 0:128], pltpu.roll(wide[:, 256:384], 128 - (YR - 256), 1)
    )
    ys = column_tiles(pad_ref, 8)
    live = iota((YR, XW), 0) < count
    top = jnp.zeros((YR, XW), F32)
    for z in range(4):
        speed = jnp.abs(v_ref[z].astype(F32)) * xs_ref[...]
        speed = speed + jnp.abs(v_ref[4 + z].astype(F32)) * ys
        top = jnp.maximum(top, speed)
    top = jnp.where(live, top, F32(0.0))
    top = jnp.max(jnp.max(top, axis=0, keepdims=True), axis=1, keepdims=True)
    last = jnp.where(row8 < 4, margin, pltpu.roll(max_tile(top), 4, 0))
    tiles = [nn(weights, v_ref[p]) for p in range(NP)]
    o_ref[0] = jnp.concatenate(tiles + [last], axis=0).astype(BF16)


def top_of(ref, first, count, stride):
    parts = [ref[pl.ds(first + j, count, stride=stride), :] for j in range(3)]
    return jnp.max(parts[0] + parts[1] + parts[2], axis=0, keepdims=True)


def x_solve_kernel(c_ref, x_ref, coupling_ref, r_ref, o_ref, a_ref, e_ref, s_ref, t_ref):
    a_ref[...] = c_ref[...].astype(F32).reshape(NCOL * 8, 128)
    part = [a_ref[pl.ds(v, NCOL, stride=8), :] for v in range(8)]
    margin = [pltpu.roll(part[6], 1, 0), pltpu.roll(part[7], 1, 0)]
    margin += [pltpu.roll(part[4], NCOL - 1, 0), pltpu.roll(part[5], NCOL - 1, 0)]
    local = x_ref[...].astype(F32)
    for k in range(2):
        for e in range(2):
            ends = part[2 * k + e]
            lane = (XW - 1) * e
            for h in range(4):
                place = 2 * HALO_X[h] + k
                ends = ends + local[place : place + 1, lane : lane + 1] * margin[h]
            e_ref[k, pl.ds(e, NCOL, stride=2), :] = ends
        s_ref[k] = nn(coupling_ref[k], e_ref[k], lax.Precision.HIGHEST)
        for e in range(2):
            a_ref[pl.ds(2 * k + e, NCOL, stride=8), :] = s_ref[k, pl.ds(e, NCOL, stride=2), :]
    for h in range(4):
        a_ref[pl.ds(4 + h, NCOL, stride=8), :] = margin[h]
    t_ref[...] = r_ref[...][:, 8 * NP : 8 * TILES, :].astype(F32).reshape(8 * NROW, 128)
    tile = max_tile(top_of(t_ref, 4, NROW, 8))
    spare = iota((8, 128), 1) >= CHUNK
    solved = a_ref[...].reshape(NCOL, 8, 128)
    o_ref[...] = jnp.where(spare[None], tile[None], solved).astype(BF16)


def y_solve_kernel(r_ref, coupling_ref, o_ref, a_ref, e_ref, s_ref, m_ref):
    a_ref[...] = r_ref[...].astype(F32).reshape(NROW * 8 * TILES, 128)

    def rows_of(place):
        return a_ref[pl.ds(place, NROW, stride=8 * TILES), :]

    source = iota((NROW, 128), 0)
    weights = [rows_of(8 * NP + j) for j in range(4)]
    weight = [
        [jnp.broadcast_to(weights[j][:, h : h + 1], (NROW, 128)) for h in range(4)]
        for j in range(4)
    ]
    for g in range(NP):
        lanes = slice(128 * g, 128 * g + 128)
        part = [rows_of(8 * g + v) for v in range(8)]
        margin = [pltpu.roll(part[6 + h], 1, 0) for h in range(2)]
        margin = [jnp.where(source == 0, F32(0.0), m) for m in margin]
        upper = [pltpu.roll(part[4 + h], NROW - 1, 0) for h in range(2)]
        margin += [jnp.where(source == NROW - 1, F32(0.0), m) for m in upper]
        for h in range(4):
            m_ref[h, :, lanes] = margin[h]
        for k in range(2):
            for e in range(2):
                ends = part[2 * k + e]
                for h in range(4):
                    ends = ends + weight[2 * k + e][h] * margin[h]
                e_ref[NP * k + g, pl.ds(e, NROW, stride=2), :] = ends
    for k in range(2):
        ends = jnp.concatenate([e_ref[NP * k + g] for g in range(NP)], axis=1)
        s_ref[k] = nn(coupling_ref[k], ends, lax.Precision.HIGHEST)
    own = row_pos()
    pieces = [s_ref[k, pl.ds(2 * own + e, 1), :] for k in range(2) for e in range(2)]
    pieces += [m_ref[h, pl.ds(own, 1), :] for h in range(4)]
    o_ref[...] = jnp.concatenate(pieces, axis=0).astype(BF16)


def own_kernel(
    count_ref, v_hbm, x_ref, xb_ref, w_ref, yb_ref, xs_ref, xv_ref, ys_ref, yc_ref,
    coef_ref, after_ref, own_ref, xc_ref, xx_ref, u_ref, hc_ref, yy_ref, xo_ref, wm_ref, v_ref, sem,
):
    fetch = pltpu.make_async_copy(v_hbm, v_ref, sem.at[0])
    fetch.start()
    count = count_ref[0:1, 0:1]
    x_all = x_ref[...]
    n_in = 2 * (XW + 4)
    dst, src = iota((XW, n_in), 0), iota((XW, n_in), 1)
    row, col = iota((8, n_in), 0), iota((8, n_in), 1)
    row_x, row_y = iota((8, XW), 0), iota((8, YR), 0)
    row_h, col_h = iota((8, YR + 4), 0), iota((8, YR + 4), 1)
    slot_in, slot_out = iota((YR + 4, YR), 0), iota((YR + 4, YR), 1)
    shift = ones_where((slot_in == slot_out + 2) & (slot_out < count)).astype(BF16)

    def placed(values, offsets):
        found = jnp.where(values[0] == 4, offsets[0], -1)
        for h in range(1, 4):
            found = jnp.where(values[0] == 4 + h, offsets[h], found)
        return ones_where(values[1] == found).astype(BF16)

    x_high = xb_ref[...].astype(BF16).astype(F32)
    y_high = yb_ref[...].astype(BF16).astype(F32)
    pick_y = placed((row_h, col_h), (0, 1, YR + 2, YR + 3))
    for k in range(2):
        lanes = slice(XW * k, XW * k + XW)
        xo_ref[:, lanes] = nn(ones_where(src == 2 * (dst + 2) + k).astype(BF16), x_all).astype(BF16)
        pick_x = placed((row, col), [2 * h + k for h in HALO_X])
        mine = (row_x // 2) == k
        head = jnp.where(mine, x_high, F32(0.0)) + nn(pick_x, x_all)
        tail = jnp.where(mine, xb_ref[...] - x_high, F32(0.0))
        xc_ref[:, lanes] = jnp.concatenate([head, tail], axis=0).astype(BF16)
        wm_ref[k] = nn(w_ref[k], shift).astype(BF16)
        mine = (row_y // 2) == k
        head = jnp.where(mine, y_high, F32(0.0)) + nt(pick_y, w_ref[k])
        tail = jnp.where(mine, yb_ref[...] - y_high, F32(0.0))
        hc_ref[k] = jnp.concatenate([head, tail], axis=0).astype(BF16)
    yy_ref[...] = jnp.zeros_like(yy_ref)
    ys = ys_ref[...].reshape(1, YR)
    yy_ref[0:1, 0:YR] = ys
    yy_ref[1:2, 0:YR] = viscosity * yc_ref[...].reshape(1, YR)
    yy_ref[2:3, 0:YR] = viscosity * ys * ys
    scale, curv, y_second = (column_tiles(yy_ref, j) for j in range(3))
    xs, xv = xs_ref[...], viscosity * xv_ref[...]
    x_second = viscosity * xs * xs
    xx_ref[...] = jnp.concatenate([xs, xv, x_second, jnp.zeros((5, XW), F32)], axis=0)
    fetch.wait()
    for z in range(4):
        u_ref[z] = v_ref[z]
    for pair in range(2):
        for f in range(3):
            plane = 4 * f + 2 * pair
            both = jnp.concatenate([v_ref[plane], v_ref[plane + 1]], axis=1)
            coef = coef_ref[:, XW * plane : XW * plane + 2 * XW].astype(F32)
            coef = jnp.concatenate([coef, coef], axis=0).astype(BF16)
            of_first = nn(wm_ref[0], both) + tn(hc_ref[0], coef)
            of_second = nn(wm_ref[1], both) + tn(hc_ref[1], coef)
            for j in range(2):
                p, z = plane + j, 2 * pair + j
                at = slice(XW * j, XW * j + XW)
                in_x = nn(v_ref[p], xo_ref[...])
                u, v = v_ref[z].astype(F32), v_ref[4 + z].astype(F32)
                rhs = (xv - u * xs) * in_x[:, 0:XW] + x_second * in_x[:, XW:]
                rhs = rhs + (curv - v * scale) * of_first[:, at]
                own_ref[p] = rhs + y_second * of_second[:, at]


def finish_kernel(
    count_ref, c_ref, v_ref, p_ref, base_ref, xc_ref, xx_ref, rhs_hbm, inc_hbm,
    x_add, t_ref, rhs_ref, inc_ref, sems,
):
    count = count_ref[0:1, 0:1]
    t_ref[...] = c_ref[...].astype(F32).reshape(8 * NCOL, 128)
    top = top_of(t_ref, 0, NCOL, 8)
    spare = iota((1, 128), 1) >= CHUNK
    top = jnp.max(jnp.where(spare, top, F32(0.0)), axis=1, keepdims=True)
    step = cfl_target / (top + 1e-06)
    gamma_step, zeta_step = gamma_coef * step, zeta_coef * step
    x_corr = xc_ref[...]
    live = iota((YR, XW), 0) < count
    xs, xv, x_second = xx_ref[0:1, :], xx_ref[1:2, :], xx_ref[2:3, :]
    done, copies = 0, []
    for p in range(NP):
        while done < CHUNKS and CHUNK * done < YR * (p + 1):
            coef = t_ref[8 * done : 8 * done + 8, :]
            coef = jnp.concatenate([coef, coef], axis=0).astype(BF16)
            x_add[CHUNK * done : CHUNK * done + 128, :] = tn(coef, x_corr)
            done += 1
        u = v_ref[p % 4].astype(F32)
        add = x_add[YR * p : YR * p + YR, :]
        rhs = (xv - u * xs) * add[:, 0:XW] + x_second * add[:, XW:]
        rhs = jnp.where(live, base_ref[p] + rhs, F32(0.0))
        before = jnp.where(live, zeta_step, F32(0.0)) * p_ref[p].astype(F32)
        rhs_ref[p] = rhs.astype(BF16)
        inc_ref[p] = (gamma_step * rhs + before).astype(BF16)
        if (p + 1) % GROUP == 0:
            group = pl.ds(p + 1 - GROUP, GROUP)
            for j, (source, target) in enumerate(((rhs_ref, rhs_hbm), (inc_ref, inc_hbm))):
                sem = sems.at[j, p // GROUP]
                copies.append(pltpu.make_async_copy(source.at[group], target.at[group], sem))
                copies[-1].start()
    for copy in copies:
        copy.wait()


VMEM = pl.BlockSpec(memory_space=pltpu.VMEM)
HBM = pl.BlockSpec(memory_space=pltpu.HBM)


def call(body, name, operands, outs, scratch=(), flops=0, mib=6, far=(), far_outs=(), alias=None):
    specs = [HBM if j in far else VMEM for j in range(len(operands))]
    size = sum(o.size * o.dtype.itemsize for o in operands)
    single = len(outs) == 1
    out_specs = [HBM if j in far_outs else VMEM for j in range(len(outs))]
    return pl.pallas_call(
        body,
        out_shape=outs[0] if single else outs,
        in_specs=specs,
        out_specs=out_specs[0] if single else out_specs,
        scratch_shapes=[pltpu.VMEM(item, F32) if isinstance(item, tuple) else item for item in scratch],
        compiler_params=pltpu.CompilerParams(vmem_limit_bytes=mib * 2**20),
        cost_estimate=pl.CostEstimate(flops=flops, bytes_accessed=size, transcendentals=0),
        input_output_aliases=alias or {},
        name=name,
    )(*operands)


def shape(dims, kind=BF16):
    return jax.ShapeDtypeStruct(dims, kind)


def shards(
    velocity, rhs_prev, row_counts, x_scale, x_curv, y_scale, y_curv,
    x_local, x_coupling, x_basis, y_local, y_coupling, y_basis,
):
    lines = velocity.reshape(LINES, XW)
    previous = rhs_prev.reshape(NP, YR, XW)
    x_rows = x_local.reshape(2 * (XW + 4), XW)
    y_mats = jnp.transpose(y_local, (1, 2, 0))
    x_scale, x_curv = x_scale.reshape(1, XW), x_curv.reshape(1, XW)

    whole = pltpu.with_memory_space_constraint(velocity.reshape(NP, YR, XW), pltpu.HBM)
    fetched = (lines, x_rows, y_mats, x_scale, y_scale)
    *fetched, row_counts = [
        pltpu.with_memory_space_constraint(item, pltpu.HBM) for item in (*fetched, row_counts)
    ]
    mine, lines, x_rows, y_mats, x_scale, y_scale, count = call(
        x_partial_kernel, "x_partial", (*fetched, row_counts),
        (
            shape((NCOL, 8, 128)), *(pltpu.VMEM(item.shape, item.dtype) for item in fetched),
            pltpu.VMEM((8, 128), jnp.int32),
        ),
        (pltpu.SMEM((NROW,), jnp.int32), pltpu.SemaphoreType.DMA((6,))),
        flops=10**8, far=range(6),
    )
    planes = lines.reshape(NP, YR, XW)
    theirs = lax.all_to_all(mine, COL, 0, 0, tiled=True)
    y_part = call(
        y_partial_kernel, "y_partial", (count, planes, y_mats, x_scale, y_scale),
        (shape((1, 8 * TILES, 128)),), ((16, 384),), flops=10**8,
    )
    columns = lax.all_gather(y_part, ROW, axis=0, tiled=True)
    x_basis = jnp.pad(x_basis.reshape(4, XW), ((0, 4), (0, 0)))
    y_basis = jnp.pad(y_basis.reshape(4, YR), ((0, 4), (0, 0)))
    x_solved = call(
        x_solve_kernel, "x_solve", (theirs, x_rows, x_coupling, columns), (shape((NCOL, 8, 128)),),
        ((NCOL * 8, 128), (2, 2 * NCOL, 128), (2, 2 * NCOL, 128), (8 * NROW, 128)), flops=10**8,
    )
    x_back = lax.all_to_all(x_solved, COL, 0, 0, tiled=True)
    wide = 128 * NP
    y_solved = call(
        y_solve_kernel, "y_solve", (columns, y_coupling), (shape((8, wide)),),
        (
            (NROW * 8 * TILES, 128), (2 * NP, 2 * NROW, 128), (2, 2 * NROW, wide), (4, NROW, wide),
        ), flops=10**8,
    )
    base, x_corr, x_lines, streamwise = call(
        own_kernel, "own",
        (
            count, whole, x_rows, x_basis, y_mats, y_basis, x_scale, x_curv, y_scale, y_curv,
            y_solved, x_solved,
        ),
        (
            shape((NP, YR, XW), F32), shape((16, 2 * XW)), shape((8, XW), F32),
            shape((4, YR, XW)),
        ),
        (
            pltpu.VMEM((2, 16, YR), BF16), (8, 384), pltpu.VMEM((XW, 2 * XW), BF16),
            pltpu.VMEM((2, YR, YR), BF16), pltpu.VMEM((NP, YR, XW), BF16),
            pltpu.SemaphoreType.DMA((1,)),
        ), flops=6 * 10**8, mib=8, far=(1, 11),
    )
    rhs, inc = call(
        finish_kernel, "finish",
        (count, x_back, streamwise, previous, base, x_corr, x_lines),
        (shape((NP, YR, XW)), shape((NP, YR, XW))),
        (
            (CHUNK * (CHUNKS - 1) + 128, 2 * XW), (8 * NCOL, 128),
            pltpu.VMEM((NP, YR, XW), BF16), pltpu.VMEM((NP, YR, XW), BF16),
            pltpu.SemaphoreType.DMA((2, NP // GROUP)),
        ), flops=10**8, mib=10, far_outs=(0, 1),
    )
    return rhs.reshape(velocity.shape), inc.reshape(velocity.shape)


def solution(mesh):
    torus = Mesh(mesh.devices.reshape(8, 2, 8, 4), ("row_0", "row_1", "col_0", "col_1"))
    placed = (
        P(None, None, ROW, COL), P(None, None, ROW, COL), P(), P(COL), P(COL), P(ROW), P(ROW),
        P(), P(), P(), P(ROW, None, None), P(), P(ROW, None, None, None),
    )
    return jax.shard_map(
        shards,
        mesh=torus,
        in_specs=placed,
        out_specs=(P(None, None, ROW, COL), P(None, None, ROW, COL)),
        check_vma=False,
    )
```
